1024 devices in a mesh: dom: 64 (over y, z), sub: 8 (over x_hi, core), lane: 2 (over x_lo).
Axes of the slice: x: 8 (x_hi: 4, x_lo: 2; x = x_hi * 2 + x_lo), y: 8, z: 8, core: 2. Of those that a mesh axis runs over, the one named last changes fastest.
Arguments:
- rhs_field: float32 [2048, 128, 256], P('dom', 'sub', 'lane'), may hold values from -6 to 6
- coef_field: float32 [2048, 128, 256], P('dom', 'sub', 'lane'), may hold values from 0.5 to 4
- pressure_old: float32 [2048, 128, 256], P('dom', 'sub', 'lane'), may hold values from -6 to 6
- cell_index: int32 [262144], P(('dom', 'sub', 'lane')), may hold values from 0 to 65535, as said below
- normals: float32 [3, 262144], P(None, ('dom', 'sub', 'lane')), may hold values from -1 to 1
- point_coords: float32 [3, 262144], P(None, ('dom', 'sub', 'lane')), may hold values from 0 to 1.8
- partner: int32 [262144, 1], P(('dom', 'sub', 'lane')), may hold values from 0 to 63; in each aligned block of 256 rows (0 to 255, 256 to 511, ...) at most 8 rows name the same one
- node_coords: float32 [3, 524288], P(None, ('dom', 'sub', 'lane')), may hold values from 0 to 1
- shell_block: float32 [524288, 512], P(('dom', 'sub', 'lane')), may hold values from -0.25 to 0.25
- disp_old: float32 [3, 262144], P(None, ('dom', 'sub', 'lane')), may hold values from -3 to 3
Outputs:
- pressure_new: float32 [2048, 128, 256], P('dom', 'sub', 'lane')
- disp_new: float32 [3, 262144], P(None, ('dom', 'sub', 'lane'))
- residual_rms: float32 [], replicated
The draws below stay inside these ranges and needn't reach their ends.
Inputs may be any that keep to these rules, and one draw needn't show every extreme that they name: `partner`: among the 256 points of one device, at most 8 name the same dom index, and that bound is reached. `cell_index`: A cell of the point's own device's block, numbered row-major over 32 x 16 x 128.
All inputs are finite; a program needn't handle non-finite values.
Results may differ from the reference program's by a relative error of at most 0.0003.
Values sent between devices are 32-bit elements; how exact they have to be, the bound alone decides.
No kernel may reach another device: no remote copies, remote signals or barrier semaphores. Data moves between devices by JAX's collectives and lax.ppermute only.
A program may use at most 32 MiB of HBM per device.

```python
import math
import jax
import jax.numpy as jnp
import numpy as np
from jax import lax

CX = 32
CY = 16
CZ = 128
SWEEPS = 4
PTS = 256
NS = 512
CAP = 8
NX = 2048
NY = 128
NZ = 256
TOTPTS = 262144
NODES = 524288
N_DOM = 64
N_SUB = 8
N_LANE = 2


def draw_cell_index(key, part):
    key = jax.random.fold_in(key, 3)
    keys = jax.random.split(key, 7)
    pos_x = jax.random.randint(keys[0], (TOTPTS,), 0, CX)
    pos_y = jax.random.randint(keys[1], (TOTPTS,), 0, CY)
    pos_z = jax.random.randint(keys[2], (TOTPTS,), 0, CZ)
    for which_key, flag_key in ((keys[3], keys[4]), (keys[5], keys[6])):
        which = jax.random.randint(which_key, (TOTPTS,), 0, 6)
        active = jax.random.randint(flag_key, (TOTPTS,), 0, 2) == 1
        side = which % 2
        facet = which // 2
        pos_x = jnp.where(active & (facet == 0), side * (CX - 1), pos_x)
        pos_y = jnp.where(active & (facet == 1), side * (CY - 1), pos_y)
        pos_z = jnp.where(active & (facet == 2), side * (CZ - 1), pos_z)
    return ((pos_x * CY + pos_y) * CZ + pos_z).astype(jnp.int32)


def draw_point_coords(key, part):
    key = jax.random.fold_in(key, 7)
    base_key, rank_key, jitter_key = jax.random.split(key, 3)
    row_of = jnp.arange(TOTPTS, dtype=jnp.int32) // (TOTPTS // N_DOM)
    ranks = jax.random.permutation(rank_key, N_DOM).astype(jnp.float32)[None, :]
    jitter = jax.random.uniform(jitter_key, (1, N_DOM), jnp.float32)
    shift = 0.8 * (ranks + jitter) / N_DOM
    base = jax.random.uniform(base_key, (3, TOTPTS), jnp.float32)
    return (base + shift[:, row_of]).astype(jnp.float32)


def levels(rng, dims, cuts, least, top_value):
    factor_of = 1.0
    for axis_at, parts in cuts:
        heights = jax.random.uniform(jax.random.fold_in(jax.random.fold_in(rng, 6), axis_at), (parts,), jnp.float32, least / len(cuts), top_value / len(cuts))
        factor_of = factor_of * jnp.repeat(jnp.exp(heights), dims[axis_at] // parts).reshape((-1,) + (1,) * (len(dims) - 1 - axis_at))
    return factor_of


def assign_block(rng, own, number, rows, number_of, top, bound, slope):
    order = jax.random.permutation(rng, number_of)
    crowded, usual = portions_of(number_of, rows * top, bound, slope, True), portions_of(number_of, rows * top, bound, slope, False)
    places = jnp.arange(number_of)

    def named(sizes, offset_by):
        used = int((sizes > 0).sum())
        fixed = max(1, used // 4)
        moved = fixed + (places - fixed + offset_by * (used - fixed)) % max(1, number_of - fixed)
        return jnp.zeros((number_of,), jnp.int32).at[order[jnp.where(places < fixed, places, moved)]].set(jnp.asarray(sizes, jnp.int32))

    sizes = jnp.where(number % 4 == 0, named(crowded, number // 4), named(usual, number - number // 4 - 1))
    mixed = jax.random.permutation(jax.random.fold_in(own, 3), number_of)
    donor, receiver = mixed[0:number_of // 2 * 2:2], mixed[1:number_of // 2 * 2:2]
    slack = jnp.minimum(sizes[donor] - 1, bound - sizes[receiver]) // 2
    slack = jnp.where((donor == order[0]) | (receiver == order[0]) | (sizes[receiver] == 0), 0, jnp.maximum(slack, 0))
    moved = jax.random.randint(jax.random.fold_in(own, 4), (number_of // 2,), 0, 1 << 20) % (slack + 1)
    sizes = sizes.at[donor].add(-moved).at[receiver].add(moved)
    labels = jnp.searchsorted(jnp.cumsum(sizes), jnp.arange(rows * top), side="right").astype(jnp.int32)
    grid = labels.reshape(top, rows).T
    grid = grid[jax.random.permutation(jax.random.fold_in(own, 1), rows)]
    offset_by = jax.random.randint(jax.random.fold_in(own, 2), (rows, 1), 0, top)
    return jnp.take_along_axis(grid, (jnp.arange(top)[None, :] + offset_by) % top, axis=1)


def portions_of(amount, total, bound, lean, full):
    weights = [(1 << 20) // math.isqrt(rank ** lean) + 1 for rank in range(1, amount + 1)]
    largest = bound if full else min(bound, max(-(-total // amount), total * weights[0] // sum(weights)))
    least = 1 if total - largest >= amount - 1 else 0
    holding, rest = [largest] + [least] * (amount - 1), total - largest - least * (amount - 1)
    while rest > 0:
        free = [i for i in range(1, amount) if holding[i] < largest] or [i for i in range(1, amount) if holding[i] < bound]
        pool, budget = sum([weights[i] for i in free]), rest
        for i in free:
            more = min(bound - holding[i], max(1, budget * weights[i] // pool), rest)
            holding[i] = holding[i] + more
            rest = rest - more
    return np.array(holding)


def scatter_about(rng, dims, width, limit, pieces=(), kind=jnp.bfloat16):
    values = jax.random.normal(rng, dims, jnp.float32) * width
    if len(pieces) > 0:
        values = levels(rng, dims, pieces, -0.22, 0.18) * values
    return jnp.clip(values, min=-limit, max=limit).astype(kind)


def setup_inputs(seed: int = 0) -> dict:
    arg_keys = jax.random.split(jax.random.key(seed), 11)
    rhs_field = scatter_about(arg_keys[0], (NX, NY, NZ), 1.0, 6.0, ((0, 64), (1, 8), (2, 2)), jnp.float32)
    coef_field = jnp.clip(jnp.exp(math.log(4.0) - 2.0794415 * jax.random.uniform(arg_keys[1], (NX, NY, NZ), jnp.float32) ** levels(arg_keys[1], (NX, NY, NZ), ((0, 64), (1, 8), (2, 2)), -0.2, 0.2)), 0.5, 4.0)
    pressure_old = scatter_about(arg_keys[2], (NX, NY, NZ), 1.0, 6.0, ((0, 64), (1, 8), (2, 2)), jnp.float32)
    cell_index = draw_cell_index(jax.random.fold_in(arg_keys[10], 71), 0)
    normals = jnp.clip(jax.random.uniform(arg_keys[4], (3, TOTPTS), jnp.float32, -1.0, 1.0) * levels(arg_keys[4], (3, TOTPTS), ((1, 1024),), -0.4, 0.0), -1.0, 1.0)
    point_coords = draw_point_coords(jax.random.fold_in(arg_keys[10], 71), 0)
    partner_keys = jax.random.split(jax.random.fold_in(arg_keys[6], 1), TOTPTS // PTS)
    partner_turns = jax.random.permutation(jax.random.fold_in(arg_keys[6], 3), TOTPTS // PTS)
    partner = jax.vmap(lambda own, number: assign_block(jax.random.fold_in(arg_keys[6], 2), own, number, PTS, N_DOM, 1, CAP, 2))(partner_keys, partner_turns).reshape((TOTPTS, 1))
    node_coords = jnp.clip(1.0 * jax.random.uniform(arg_keys[7], (3, NODES), jnp.float32) ** levels(arg_keys[7], (3, NODES), ((1, 1024),), -0.2, 0.2), 0.0, 1.0)
    shell_block = scatter_about(arg_keys[8], (NODES, NS), NS ** -0.5, 0.25, ((0, 1024),), jnp.float32)
    disp_old = scatter_about(arg_keys[9], (3, TOTPTS), 0.5, 3.0, ((1, 1024),), jnp.float32)
    return dict(rhs_field=rhs_field, coef_field=coef_field, pressure_old=pressure_old, cell_index=cell_index, normals=normals, point_coords=point_coords, partner=partner, node_coords=node_coords, shell_block=shell_block, disp_old=disp_old)


source_gain = 16.0
relaxation = 0.5
inv_radius_sq = 11.111111
epsilon = 1e-06

def neighbours(padded):
    total = padded[2:, 1:-1, 1:-1] + padded[:-2, 1:-1, 1:-1]
    total = total + padded[1:-1, 2:, 1:-1] + padded[1:-1, :-2, 1:-1]
    total = total + padded[1:-1, 1:-1, 2:] + padded[1:-1, 1:-1, :-2]
    return total

def slot_of(target):
    onehot = (target[:, None] == jnp.arange(N_DOM, dtype=jnp.int32)[None, :]).astype(jnp.int32)
    slot_rank = lax.optimization_barrier(jnp.sum((jnp.cumsum(onehot, axis=0) - onehot) * onehot, axis=1))
    return (target * CAP + slot_rank).astype(jnp.int32)

def structure(items):
    received, nodes, shell = items
    coords = received[:3]
    forces = received[3:]
    distance = jnp.zeros((coords.shape[1], nodes.shape[1]), jnp.float32)
    for comp in range(3):
        distance = distance + (coords[comp][:, None] - nodes[comp][None, :]) ** 2
    kernel = jnp.exp(-distance * inv_radius_sq)
    loading = jnp.dot(forces, kernel, precision=lax.Precision.HIGHEST) / math.sqrt(PTS)
    displaced = loading + jnp.dot(loading, shell, precision=lax.Precision.HIGHEST)
    return jnp.dot(displaced, kernel.T, precision=lax.Precision.HIGHEST) / math.sqrt(NS)

def add_at(block, index, values):
    return block.at[index].add(values)

def fill_slots(payload, slot_index):
    return jnp.zeros((payload.shape[0], N_DOM * CAP), jnp.float32).at[:, slot_index].set(payload)

def reference(rhs_field, coef_field, pressure_old, cell_index, normals, point_coords, partner, node_coords, shell_block, disp_old):
    dev_count = N_DOM * N_SUB * N_LANE

    def to_blocks(field):
        return field.reshape(N_DOM, CX, N_SUB, CY, N_LANE, CZ).transpose(0, 2, 4, 1, 3, 5).reshape(dev_count, CX * CY * CZ)

    def from_blocks(blocks):
        return blocks.reshape(N_DOM, N_SUB, N_LANE, CX, CY, CZ).transpose(0, 3, 1, 4, 2, 5).reshape(N_DOM * CX, N_SUB * CY, N_LANE * CZ)

    def per_point(array):
        return array.reshape(3, dev_count, PTS).transpose(1, 0, 2)
    cells = cell_index.reshape(dev_count, PTS)
    slots = jax.vmap(slot_of)(partner.reshape(dev_count, PTS))
    nodes = node_coords.reshape(3, dev_count, NS).transpose(1, 0, 2)
    shells = shell_block.reshape(dev_count, NS, NS)
    norm_pts = per_point(normals)
    coord_pts = per_point(point_coords)
    rhs_blocks = to_blocks(rhs_field)
    denom = 6.0 + coef_field

    def fluid_solve(source_field):
        pressure = pressure_old
        for sweep_no in range(SWEEPS):
            pressure = (source_field + neighbours(jnp.pad(pressure, 1))) / denom
        return pressure

    def couple(disp):
        values = source_gain * lax.optimization_barrier(jnp.sum(disp * norm_pts, axis=1))
        source_blocks = jax.vmap(add_at)(rhs_blocks, cells, values)
        pressure = fluid_solve(from_blocks(source_blocks))
        press_pts = jnp.take_along_axis(to_blocks(pressure), cells, axis=1)
        force = press_pts[:, None, :] * norm_pts
        payload = jnp.concatenate([coord_pts, force], axis=1)
        sent = jax.vmap(fill_slots)(payload, slots)
        received = sent.reshape(N_DOM, N_SUB * N_LANE, 6, N_DOM, CAP).transpose(3, 1, 2, 0, 4).reshape(dev_count, 6, N_DOM * CAP)
        returned = lax.map(structure, (received, nodes, shells))
        arrived = returned.reshape(N_DOM, N_SUB * N_LANE, 3, N_DOM, CAP).transpose(3, 1, 2, 0, 4).reshape(dev_count, 3, N_DOM * CAP)
        index = jnp.broadcast_to(slots[:, None, :], (dev_count, 3, PTS))
        return (pressure, jnp.take_along_axis(arrived, index, axis=2))
    first = per_point(disp_old)
    pressure_a, mapped_a = couple(first)
    resid_a = mapped_a - first
    second = first + relaxation * resid_a
    pressure_new, mapped_b = couple(second)
    resid_b = mapped_b - second
    delta = resid_b - resid_a
    dot_vr = jnp.sum(delta * resid_b)
    dot_vv = jnp.sum(delta * delta)
    dot_rr = jnp.sum(resid_b * resid_b)
    weight_iqn = dot_vr / (dot_vv + epsilon)
    updated = mapped_b - weight_iqn * (mapped_b - mapped_a)
    disp_new = updated.transpose(1, 0, 2).reshape(3, dev_count * PTS)
    residual_rms = jnp.sqrt(dot_rr / (3.0 * dev_count * PTS))
    return (pressure_new, disp_new, residual_rms)
```

```python
import math

import jax
import jax.numpy as jnp
from jax import lax
from jax.experimental import pallas as pl
from jax.experimental.pallas import tpu as pltpu
from jax.sharding import PartitionSpec as P

SWEEPS = 4
DOM, SUB, LANE = 64, 8, 2
CX, CY, CZ = 32, 16, 128
PTS, NS, CAP = 256, 512, 8
RX, RY = CX + 8, CY + 8
WIDE = 16

source_gain = 16.0
relaxation = 0.5
inv_radius_sq = 11.111111
epsilon = 1e-06

f32, bf16, i32 = jnp.float32, jnp.bfloat16, jnp.int32
NN = (((1,), (0,)), ((), ()))
NT = (((1,), (1,)), ((), ()))


def pieces(x, count):
    parts = []
    for _ in range(count - 1):
        head = x.astype(bf16)
        parts.append(head)
        x = x - head.astype(f32)
    parts.append(x.astype(bf16))
    return parts


def mxu(a, b, dims):
    return lax.dot_general(a, b, dims, preferred_element_type=f32)


def ones_at(rows, index):
    at = lax.broadcasted_iota(i32, (rows, index.shape[1]), 0)
    return at == index


def as_ones(mask):
    return jnp.where(mask, 1.0, 0.0).astype(bf16)


def spread(row_mask, z, values):
    weights = jnp.where(ones_at(CZ, z), values, 0.0)
    rows = as_ones(row_mask)
    total = None
    for part in pieces(weights, 3):
        term = mxu(rows, part, NT)
        total = term if total is None else total + term
    return total


def halves(row):
    return row[:, 0:128], row[:, 128:256]


def joined(ref_rows):
    return jnp.concatenate([ref_rows[0:1], ref_rows[1:2]], axis=1)


def start_kernel(rhs, coef, pold, cell, part, nrm, disp, src, rden, low, high, slot):
    points = cell[...]
    values = source_gain * jnp.sum(disp[...] * nrm[...], axis=0, keepdims=True)
    added = spread(ones_at(CX * CY, points >> 7), points & 127, values)
    src[...] = rhs[...] + added.reshape(CX, CY, CZ)
    rden[...] = 1.0 / (6.0 + coef[...])
    owner = ones_at(DOM, part[...])
    earlier = lax.broadcasted_iota(i32, (PTS, PTS), 0) < lax.broadcasted_iota(i32, (PTS, PTS), 1)
    before = mxu(as_ones(owner), as_ones(earlier), NN)
    rank = jnp.sum(jnp.where(owner, before, 0.0), axis=0, keepdims=True)
    slots = part[...].astype(f32) * CAP + rank
    slot[...] = slots
    for out, first in ((low, 0), (high, CX)):
        base3 = 0 if first == 0 else CX - 3
        base4 = 0 if first == 0 else CX - 4
        out[0:3] = src[base3 : base3 + 3]
        out[3:6] = rden[base3 : base3 + 3]
        out[6:10] = pold[base4 : base4 + 4]
        out[10] = jnp.zeros((CY, CZ), f32)
        for at, row in enumerate((*halves(points.astype(f32)), *halves(slots))):
            out[10, at : at + 1, :] = row


def sub_kernel(src, rden, pold, cell, fromhigh, fromlow, low, high):
    for out, base3, base4 in ((low, 0, 0), (high, CY - 3, CY - 4)):
        for field, own, width, base in ((0, src, 3, base3), (3, rden, 3, base3), (6, pold, 4, base4)):
            for k in range(width):
                y = base + k
                out[field + k, 0:CX, :] = own[:, y, :]
                rows_high = fromhigh[field : field + width, y, :]
                rows_low = fromlow[field : field + width, y, :]
                if width == 3:
                    gap = jnp.zeros((2, CZ), f32)
                    rest = jnp.concatenate([rows_high, gap, rows_low], axis=0)
                else:
                    rest = jnp.concatenate([rows_high, rows_low], axis=0)
                out[field + k, CX:RX, :] = rest
        out[10] = jnp.zeros((RX, CZ), f32)
        a, b = halves(cell[...].astype(f32))
        out[10, 0:1, :] = a
        out[10, 1:2, :] = b
        out[10, 2:4, :] = fromhigh[10, 0:2, :]
        out[10, 4:6, :] = fromlow[10, 0:2, :]


def lane_kernel(place, src, rden, pold, cell, fromhigh, fromlow, subhigh, sublow, esrc, erden, epold, strips, meta):
    for field, own, width, ext in ((0, src, 3, esrc), (3, rden, 3, erden), (6, pold, 4, epold)):
        ext[0:CX, 0:CY, :] = own[...]
        ext[CX : CX + width, 0:CY, :] = fromhigh[field : field + width]
        ext[RX - width : RX, 0:CY, :] = fromlow[field : field + width]
        if width == 3:
            ext[CX + 3 : CX + 5, 0:CY, :] = jnp.zeros((2, CY, CZ), f32)
            ext[:, CY + 3, :] = jnp.zeros((RX, CZ), f32)
            ext[:, CY + 4, :] = jnp.zeros((RX, CZ), f32)
        for k in range(width):
            ext[:, CY + k, :] = subhigh[field + k]
            ext[:, RY - width + k, :] = sublow[field + k]
    lane = place[1]
    shift = jnp.where(lane == 0, 4, 0)
    at = lax.broadcasted_iota(i32, (RY, CZ), 1)
    group = RX // 8
    for x in range(group):
        total = jnp.zeros((RY, CZ), f32)
        for k in range(8):
            for field, ext in enumerate((esrc, erden, epold)):
                lo = 16 * k + 4 * field
                moved = pltpu.roll(ext[k * group + x], lax.rem(lo + shift, 128), 1)
                total = jnp.where((at >= lo) & (at < lo + 4), moved, total)
        strips[x] = total
    meta[...] = jnp.zeros((RY, CZ), f32)
    a, b = halves(cell[...].astype(f32))
    meta[0:1, :] = a
    meta[1:2, :] = b
    meta[2:4, :] = fromhigh[10, 0:2, :]
    meta[4:6, :] = fromlow[10, 0:2, :]
    meta[6:12, :] = subhigh[10, 0:6, :]
    meta[12:18, :] = sublow[10, 0:6, :]
    strips[group] = meta[...]


def sweeps(source, scale, first, even, odd):
    held = first
    for number in range(SWEEPS):
        out = even if number % 2 == 0 else odd
        now = held

        def chunk(i, _, now=now, out=out):
            base = i * 8
            window = [now[lax.rem(base + RX - 1 + k, RX)] for k in range(10)]
            for k in range(8):
                x = base + k
                here = window[k + 1]
                total = window[k + 2] + window[k]
                total = total + (pltpu.roll(here, RY - 1, 0) + pltpu.roll(here, 1, 0))
                total = total + (pltpu.roll(here, 2 * CZ - 1, 1) + pltpu.roll(here, 1, 1))
                out[x] = (source[x] + total) * scale[x]
            return 0

        lax.fori_loop(0, RX // 8, chunk, 0)
        held = out
    return held


def at_points(pressure, points):
    flat = pressure.reshape(CX * CY, CZ).T
    rows = as_ones(ones_at(CX * CY, points >> 7))
    total = None
    for part in pieces(flat, 3):
        term = mxu(part, rows, NN)
        total = term if total is None else total + term
    return jnp.sum(jnp.where(ones_at(CZ, points & 127), total, 0.0), axis=0, keepdims=True)


def to_slots(values, slots):
    rank = slots & 7
    filler = [jnp.zeros((1, PTS), f32)] * (WIDE - len(values))
    block = jnp.concatenate(list(values) + filler, axis=0)
    stacked = jnp.concatenate([jnp.where(rank == r, block, 0.0) for r in range(CAP)], axis=0)
    owner = as_ones(ones_at(DOM, slots >> 3))
    total = None
    for part in pieces(stacked, 3):
        term = mxu(owner, part, NT)
        total = term if total is None else total + term
    return total


def from_slots(arrived, slots):
    rank = slots & 7
    owner = as_ones(ones_at(DOM, slots >> 3))
    flat = arrived.T
    total = None
    for part in pieces(flat, 3):
        term = mxu(part, owner, NN)
        total = term if total is None else total + term
    found = jnp.zeros((WIDE, PTS), f32)
    for r in range(CAP):
        found = found + jnp.where(rank == r, total[r * WIDE : (r + 1) * WIDE], 0.0)
    return found


def forces_at(pressure, points, nrm):
    press = at_points(pressure, points)
    return [press * nrm[c : c + 1, :] for c in range(3)]


def first_fluid_kernel(
    place, esrc, erden, epold, strips, cell, nrm, coords, disp, slot, fsrc, frden, fpold, sending, even, odd
):
    lane = place[1]
    at = lax.broadcasted_iota(i32, (RY, CZ), 1)
    keep = jnp.where(lane == 0, at, CZ - 1 - at) < 4
    group = RX // 8
    for field, (ext, full) in enumerate(((esrc, fsrc), (erden, frden), (epold, fpold))):
        full[:, :, 0:CZ] = ext[...]
        for x in range(group):
            packed = strips[x]
            for k in range(8):
                lo = 16 * k + 4 * field
                moved = pltpu.roll(packed, lax.rem(256 - lo - 4 * lane, 128), 1)
                full[k * group + x, :, CZ : 2 * CZ] = jnp.where(keep, moved, 0.0)
    held = sweeps(fsrc, frden, fpold, even, odd)
    slots = slot[...].astype(i32)
    values = forces_at(held[0:CX, 0:CY, 0:CZ], cell[...], nrm)
    values += [coords[c : c + 1, :] for c in range(3)]
    values += [disp[c : c + 1, :] for c in range(3)]
    values += [nrm[c : c + 1, :] for c in range(3)]
    values += [jnp.ones((1, PTS), f32)]
    sending[...] = to_slots(values, slots)


def second_fluid_kernel(
    place, fsrc, frden, fpold, arrived, meta, strips, cell, nrm, slot, pressure, sending, source, even, odd
):
    sub, lane = place[0], place[1]
    source[...] = fsrc[...]
    for tile in range(2):
        cells_of = meta if tile == 0 else strips.at[RX // 8]
        other = jnp.where(tile == 0, lane, 1 - lane)
        lanes = slice(tile * CZ, (tile + 1) * CZ)
        beside_x = jnp.zeros((8 * CY, CZ), f32)
        beside_y = jnp.zeros((CX * 8, CZ), f32)
        corner = jnp.zeros((64, CZ), f32)
        for dy, off_y in enumerate((0, 1, -1)):
            wanted = sub + off_y
            inside = (wanted >= 0) & (wanted < SUB)
            block = arrived[lax.rem(wanted + SUB, SUB) * LANE + other]
            block = jnp.where(inside, block, 0.0)
            for dx in range(3):
                values = joined(block[2 * dx : 2 * dx + 2])
                at = (dy * 3 + dx) * 2
                points = joined(cells_of[at : at + 2, :]).astype(i32)
                x, y, z = points >> 11, (points >> 7) & 15, points & 127
                if dx == 1:
                    x = jnp.where(x < 3, x, -1000)
                elif dx == 2:
                    x = jnp.where(x >= CX - 3, x - (CX - 8), -1000)
                if dy == 1:
                    y = jnp.where(y < 3, y, -1000000)
                elif dy == 2:
                    y = jnp.where(y >= CY - 3, y - (CY - 8), -1000000)
                if dx == 0 and dy == 0:
                    added = spread(ones_at(CX * CY, points >> 7), z, values)
                    source[0:CX, 0:CY, lanes] += added.reshape(CX, CY, CZ)
                elif dy == 0:
                    beside_x = beside_x + spread(ones_at(8 * CY, x * CY + y), z, values)
                elif dx == 0:
                    beside_y = beside_y + spread(ones_at(CX * 8, x * 8 + y), z, values)
                else:
                    corner = corner + spread(ones_at(64, x * 8 + y), z, values)
        source[CX:RX, 0:CY, lanes] += beside_x.reshape(8, CY, CZ)
        source[0:CX, CY:RY, lanes] += beside_y.reshape(CX, 8, CZ)
        source[CX:RX, CY:RY, lanes] += corner.reshape(8, 8, CZ)
    held = sweeps(source, frden, fpold, even, odd)
    own = held[0:CX, 0:CY, 0:CZ]
    pressure[...] = own
    sending[...] = to_slots(forces_at(own, cell[...], nrm), slot[...].astype(i32))


def by_slot(received):
    flat = received.T
    return jnp.concatenate([flat[r * WIDE : (r + 1) * WIDE] for r in range(CAP)], axis=1)


def by_row(values):
    flat = jnp.concatenate([values[:, r * DOM : (r + 1) * DOM] for r in range(CAP)], axis=0)
    return flat.T


def product(left, head, tail, dims):
    a, b = pieces(left, 2)
    rows = left.shape[0]
    both = mxu(jnp.concatenate([a, b], axis=0), head, dims)
    return both[:rows] + both[rows:] + mxu(a, tail, dims)


def mapped_back(forces, khead, ktail, shell):
    loading = product(forces, khead, ktail, NN) * (1.0 / math.sqrt(PTS))
    shead, stail = pieces(shell, 2)
    displaced = loading + product(loading, shead, stail, NN)
    return product(displaced, khead, ktail, NT) * (1.0 / math.sqrt(NS))


def first_structure_kernel(received, nodes, shell, returned, mapped, khead, ktail):
    for r in range(CAP):
        distance = None
        for c in range(3):
            lane = r * WIDE + 3 + c
            gap = received[:, lane : lane + 1] - nodes[c : c + 1, :]
            distance = gap * gap if distance is None else distance + gap * gap
        weight = jnp.exp(-distance * inv_radius_sq)
        head, tail = pieces(weight, 2)
        khead[r * DOM : (r + 1) * DOM, :] = head
        ktail[r * DOM : (r + 1) * DOM, :] = tail
    held = by_slot(received[...])
    back = mapped_back(held[0:WIDE], khead[...], ktail[...], shell[...])
    mapped[...] = back
    moved = (source_gain * relaxation) * jnp.sum(held[9:12] * (back[0:3] - held[6:9]), axis=0, keepdims=True)
    rows = jnp.concatenate([moved, jnp.zeros((WIDE - 1, NS), f32)], axis=0)
    own = by_row(rows)
    at = lax.broadcasted_iota(i32, own.shape, 0)
    above = jnp.where(at == DOM - 1, 0.0, pltpu.roll(own, DOM - 1, 0))
    below = jnp.where(at == 0, 0.0, pltpu.roll(own, 1, 0))
    returned[...] = own + pltpu.roll(above, 1, 1) + pltpu.roll(below, 2, 1)


def second_structure_kernel(received, before, mapped, khead, ktail, shell, returned):
    forces = by_slot(received[...])
    held = by_slot(before[...])
    back = mapped_back(forces, khead[...], ktail[...], shell[...])
    t0, t1, d0, used = mapped[0:3, :], back[0:3], held[6:9], held[12:13]
    r0 = t0 - d0
    r1 = t1 - (d0 + relaxation * r0)
    delta = r1 - r0
    sums = []
    for term in (delta * r1, delta * delta, r1 * r1):
        inner = jnp.sum(term * used, axis=0, keepdims=True)
        sums.append(jnp.broadcast_to(jnp.sum(inner, axis=1, keepdims=True), (1, NS)))
    rows = jnp.concatenate([t1, t0, *sums, jnp.zeros((WIDE - 9, NS), f32)], axis=0)
    returned[...] = by_row(rows)


def hand_out_kernel(arrived, slot, high, low, out):
    held = arrived[...]
    rows = []
    for block in range(3):
        if block == 0:
            slots = slot[...]
        else:
            slots = joined((high if block == 1 else low)[10, 2:4, :])
        found = from_slots(held, slots.astype(i32))
        rows += halves(found[block : block + 1])
    rows += [jnp.zeros((2, 128), f32)]
    payload = jnp.concatenate(rows, axis=0)
    for k in range(SUB * LANE):
        out[k] = payload


def arrive_kernel(arrived, slot, found, out):
    held = arrived[...]
    found[...] = from_slots(held, slot[...].astype(i32))
    total = jnp.sum(held, axis=0, keepdims=True)
    for k in range(SUB * LANE):
        out[k : k + 1, :] = total


def finish_kernel(found, sums, disp, rms):
    total = jnp.sum(sums[...], axis=0, keepdims=True)
    vr, vv, rr = total[:, 6:7], total[:, 7:8], total[:, 8:9]
    t1, t0 = found[0:3, :], found[3:6, :]
    disp[...] = t1 - (vr / (vv + epsilon)) * (t1 - t0)
    count = 3.0 * PTS * DOM * SUB * LANE
    rms[...] = jnp.sqrt(rr / count)


def shape(*dims, dtype=f32):
    return jax.ShapeDtypeStruct(dims, dtype)


def call(kernel, outs, args, scratch=(), scalars=0, name=None):
    specs = [pl.BlockSpec(memory_space=pltpu.SMEM)] * scalars
    specs += [pl.BlockSpec(memory_space=pltpu.VMEM)] * (len(args) - scalars)
    return pl.pallas_call(
        kernel,
        out_shape=outs,
        in_specs=specs,
        out_specs=jax.tree.map(lambda _: pl.BlockSpec(memory_space=pltpu.VMEM), outs),
        scratch_shapes=list(scratch),
        compiler_params=pltpu.CompilerParams(vmem_limit_bytes=40 * 1024 * 1024),
        name=name,
    )(*args)


def body(rhs, coef, pold, cell_index, nrm, coords, partner, nodes, shell, disp):
    place = jnp.stack([lax.axis_index("sub"), lax.axis_index("lane")]).astype(i32)
    cell = cell_index.reshape(1, PTS)
    part = partner.reshape(1, PTS)
    block, field = shape(CX, CY, CZ), shape(RX, RY, 2 * CZ)
    row = shape(DOM, CAP * WIDE)

    def pair(low, high, axis):
        count = lax.axis_size(axis)
        fromhigh = lax.ppermute(low, axis, [(i + 1, i) for i in range(count - 1)])
        fromlow = lax.ppermute(high, axis, [(i, i + 1) for i in range(count - 1)])
        return fromhigh, fromlow

    def across(rows):
        return lax.all_to_all(rows, "dom", 0, 0, tiled=True)

    slab, face = shape(11, CY, CZ), shape(11, RX, CZ)
    src, rden, low, high, slot = call(
        start_kernel, (block, block, slab, slab, shape(1, PTS)), (rhs, coef, pold, cell, part, nrm, disp), name="start"
    )
    fromhigh, fromlow = pair(low, high, "dom")
    low, high = call(sub_kernel, (face, face), (src, rden, pold, cell, fromhigh, fromlow), name="sub_faces")
    subhigh, sublow = pair(low, high, "sub")
    half = shape(RX, RY, CZ)
    esrc, erden, epold, strips, meta = call(
        lane_kernel,
        (half, half, half, shape(RX // 8 + 1, RY, CZ), shape(RY, CZ)),
        (place, src, rden, pold, cell, fromhigh, fromlow, subhigh, sublow),
        scalars=1,
        name="lane_faces",
    )
    strips = lax.ppermute(strips, "lane", [(0, 1), (1, 0)])
    grids = [pltpu.VMEM((RX, RY, 2 * CZ), f32)] * 2
    fsrc, frden, fpold, sending = call(
        first_fluid_kernel,
        (field, field, field, row),
        (place, esrc, erden, epold, strips, cell, nrm, coords, disp, slot),
        grids,
        scalars=1,
        name="first_fluid",
    )
    received = across(sending)
    square = shape(NS, NS, dtype=bf16)
    returned, mapped, khead, ktail = call(
        first_structure_kernel, (row, shape(WIDE, NS), square, square), (received, nodes, shell), name="first_structure"
    )
    arrived = across(returned)
    (spread_out,) = call(
        hand_out_kernel, (shape(SUB * LANE, 8, 128),), (arrived, slot, fromhigh, fromlow), name="hand_out"
    )
    values = lax.all_to_all(spread_out, ("sub", "lane"), 0, 0, tiled=True)
    pressure, sending = call(
        second_fluid_kernel,
        (block, row),
        (place, fsrc, frden, fpold, values, meta, strips, cell, nrm, slot),
        grids + [pltpu.VMEM((RX, RY, 2 * CZ), f32)],
        scalars=1,
        name="second_fluid",
    )
    again = across(sending)
    (returned,) = call(
        second_structure_kernel, (row,), (again, received, mapped, khead, ktail, shell), name="second_structure"
    )
    arrived = across(returned)
    found, sums = call(
        arrive_kernel, (shape(WIDE, PTS), shape(SUB * LANE, 128)), (arrived, slot), name="arrive"
    )
    sums = lax.all_to_all(sums, ("sub", "lane"), 0, 0, tiled=True)
    disp_new, rms = call(finish_kernel, (shape(3, PTS), shape(1, 1)), (found, sums), name="finish")
    return pressure, disp_new, rms.reshape(())


def solution(mesh):
    every = ("dom", "sub", "lane")
    grid, points = P(*every), P(None, every)
    return jax.shard_map(
        body,
        mesh=mesh,
        in_specs=(grid, grid, grid, P(every), points, points, P(every, None), points, P(every, None), points),
        out_specs=(grid, points, P()),
        check_vma=False,
    )
```

```python
import math

import jax
import jax.numpy as jnp
from jax import lax
from jax.experimental import pallas as pl
from jax.experimental.pallas import tpu as pltpu
from jax.sharding import PartitionSpec as P

SWEEPS = 4
DOM, SUB, LANE = 64, 8, 2
CX, CY, CZ = 32, 16, 128
PTS, NS, CAP = 256, 512, 8
RX, RY = CX + 8, CY + 8
WIDE = 16

source_gain = 16.0
relaxation = 0.5
inv_radius_sq = 11.111111
epsilon = 1e-06

f32, bf16, i32 = jnp.float32, jnp.bfloat16, jnp.int32
NN = (((1,), (0,)), ((), ()))
NT = (((1,), (1,)), ((), ()))


def pieces(x, count):
    parts = []
    for _ in range(count - 1):
        head = x.astype(bf16)
        parts.append(head)
        x = x - head.astype(f32)
    parts.append(x.astype(bf16))
    return parts


def mxu(a, b, dims):
    return lax.dot_general(a, b, dims, preferred_element_type=f32)


def ones_at(rows, index):
    at = lax.broadcasted_iota(i32, (rows, index.shape[1]), 0)
    return at == index


def as_ones(mask):
    return jnp.where(mask, 1.0, 0.0).astype(bf16)


def spread(rows, z, values, edge=None):
    if edge is None:
        parts = pieces(jnp.where(ones_at(CZ, z), values, 0.0), 3)
    else:
        near = jnp.where(edge == 0, z, z - (CZ - 16))
        parts = []
        for part in pieces(jnp.where(ones_at(16, near), values, 0.0), 3):
            zero = jnp.zeros_like(part)
            first, last = jnp.where(edge == 0, part, zero), jnp.where(edge == 0, zero, part)
            parts.append(jnp.concatenate([first, jnp.zeros((CZ - 32, PTS), bf16), last], axis=0))
    total = None
    for part in parts:
        term = mxu(rows, part, NT)
        total = term if total is None else total + term
    return total


def halves(row):
    return row[:, 0:128], row[:, 128:256]


def joined(ref_rows):
    return jnp.concatenate([ref_rows[0:1], ref_rows[1:2]], axis=1)


def start_kernel(
    rhs_far, coef_far, pold_far, cell_far, part_far, nrm_far, disp_far,
    src, rden, pold, low, high, slot, cell, nrm, disp, rhs, coef, part, sems,
):
    pairs = (
        (cell_far, cell), (part_far, part), (nrm_far, nrm), (disp_far, disp),
        (rhs_far, rhs), (pold_far, pold), (coef_far, coef),
    )
    copies = [pltpu.make_async_copy(a, b, sems.at[k]) for k, (a, b) in enumerate(pairs)]
    for copy in copies:
        copy.start()
    for copy in copies[:4]:
        copy.wait()
    points = cell[...]
    values = source_gain * jnp.sum(disp[...] * nrm[...], axis=0, keepdims=True)
    added = spread(as_ones(ones_at(CX * CY, points >> 7)), points & 127, values)
    owner = ones_at(DOM, part[...])
    earlier = lax.broadcasted_iota(i32, (PTS, PTS), 0) < lax.broadcasted_iota(i32, (PTS, PTS), 1)
    before = mxu(as_ones(owner), as_ones(earlier), NN)
    rank = jnp.sum(jnp.where(owner, before, 0.0), axis=0, keepdims=True)
    slot[...] = part[...].astype(f32) * CAP + rank
    copies[4].wait()
    src[...] = rhs[...] + added.reshape(CX, CY, CZ)
    copies[6].wait()
    rden[...] = 1.0 / (6.0 + coef[...])
    copies[5].wait()
    tail = jnp.concatenate([*halves(points.astype(f32)), jnp.zeros((6, CZ), f32)], axis=0)
    for out, base3, base4 in ((low, 0, 0), (high, CY - 3, CY - 4)):
        for field, own, width, base in ((0, src, 3, base3), (3, rden, 3, base3), (6, pold, 4, base4)):
            for k in range(width):
                at = (field + k) * CX
                out[at : at + CX, :] = own[:, base + k, :]
        out[10 * CX : 10 * CX + 8, :] = tail


def dom_kernel(src, rden, pold, cell, slot, subhigh, sublow, low, high):
    tail = jnp.concatenate(
        [
            *halves(cell[...].astype(f32)),
            subhigh[10 * CX : 10 * CX + 2],
            sublow[10 * CX : 10 * CX + 2],
            *halves(slot[...]),
        ],
        axis=0,
    )
    for out, base3, base4 in ((low, 0, 0), (high, CX - 3, CX - 4)):
        for field, own, width, base in ((0, src, 3, base3), (3, rden, 3, base3), (6, pold, 4, base4)):
            for k in range(width):
                x, at = base + k, (field + k) * RY
                out[at : at + CY, :] = own[x]
                rows = [subhigh[(field + j) * CX + x : (field + j) * CX + x + 1] for j in range(width)]
                rows += [jnp.zeros((1, CZ), f32)] * (8 - 2 * width)
                rows += [sublow[(field + j) * CX + x : (field + j) * CX + x + 1] for j in range(width)]
                out[at + CY : at + RY, :] = jnp.concatenate(rows, axis=0)
        out[10 * RY : 10 * RY + 8, :] = tail


def lane_kernel(place, src, rden, pold, cell, subhigh, sublow, domhigh, domlow, esrc, erden, epold, strips, meta):
    for field, own, width, ext in ((0, src, 3, esrc), (3, rden, 3, erden), (6, pold, 4, epold)):
        ext[0:CX, 0:CY, :] = own[...]
        if width == 3:
            ext[0:CX, CY:RY, :] = jnp.zeros((CX, 8, CZ), f32)
            ext[CX + 3 : CX + 5] = jnp.zeros((2, RY, CZ), f32)
        for k in range(width):
            at = (field + k) * CX
            ext[0:CX, CY + k, :] = subhigh[at : at + CX]
            ext[0:CX, RY - width + k, :] = sublow[at : at + CX]
            at = (field + k) * RY
            ext[CX + k] = domhigh[at : at + RY]
            ext[RX - width + k] = domlow[at : at + RY]
    lane = place[1]
    shift = jnp.where(lane == 0, 4, 0)
    at = lax.broadcasted_iota(i32, (RY, CZ), 1)
    group = RX // 8
    for x in range(group):
        total = jnp.zeros((RY, CZ), f32)
        for k in range(8):
            for field, ext in enumerate((esrc, erden, epold)):
                lo = 16 * k + 4 * field
                moved = pltpu.roll(ext[k * group + x], lax.rem(lo + shift, 128), 1)
                total = jnp.where((at >= lo) & (at < lo + 4), moved, total)
        strips[x] = total
    a, b = halves(cell[...].astype(f32))
    cells = [a, b, subhigh[10 * CX : 10 * CX + 2], sublow[10 * CX : 10 * CX + 2]]
    cells += [domhigh[10 * RY : 10 * RY + 6], domlow[10 * RY : 10 * RY + 6], jnp.zeros((6, CZ), f32)]
    cells = jnp.concatenate(cells, axis=0)
    meta[...] = cells
    strips[group] = cells


def sweep(now, out, source, scale):
    def chunk(i, _):
        base = i * 8

        def at(pair, x):
            return jnp.concatenate([pair[0][x], pair[1][x]], axis=1)

        window = [at(now, lax.rem(base + RX - 1 + k, RX)) for k in range(10)]
        for k in range(8):
            x = base + k
            here = window[k + 1]
            total = window[k + 2] + window[k]
            total = total + (pltpu.roll(here, RY - 1, 0) + pltpu.roll(here, 1, 0))
            total = total + (pltpu.roll(here, 2 * CZ - 1, 1) + pltpu.roll(here, 1, 1))
            total = (at(source, x) + total) * at(scale, x)
            out[0][x], out[1][x] = total[:, 0:CZ], total[:, CZ : 2 * CZ]
        return 0

    lax.fori_loop(0, RX // 8, chunk, 0)


def last_sweep(now, source, scale, write):
    def chunk(i, _):
        base = i * 8
        window = [now[0][lax.rem(base + RX - 1 + k, RX)] for k in range(10)]
        for k in range(8):
            x = base + k
            here = window[k + 1]
            total = window[k + 2] + window[k]
            total = total + (pltpu.roll(here, RY - 1, 0) + pltpu.roll(here, 1, 0))
            wide = jnp.concatenate([here[0:CY], now[1][x, 0:CY]], axis=1)
            beside = pltpu.roll(wide, 2 * CZ - 1, 1) + pltpu.roll(wide, 1, 1)
            total = total[0:CY] + beside[:, 0:CZ]
            write(x, (source[0][x, 0:CY] + total) * scale[0][x, 0:CY])
        return 0

    lax.fori_loop(0, CX // 8, chunk, 0)


def forces_at(pressure, points, nrm):
    at_z = as_ones(ones_at(CZ, points & 127))
    total = None
    for part in pieces(pressure, 3):
        term = mxu(part, at_z, NN)
        total = term if total is None else total + term
    press = jnp.sum(jnp.where(ones_at(CX * CY, points >> 7), total, 0.0), axis=0, keepdims=True)
    return [press * nrm[c : c + 1, :] for c in range(3)]


def first_fluid_kernel(
    place, esrc, erden, epold, strips, cell, nrm, coords, disp, slot,
    pressure, xrden, sending, xsrc, xpold, even0, even1, odd0, odd1,
):
    lane = place[1]
    at = lax.broadcasted_iota(i32, (RY, CZ), 1)
    keep = jnp.where(lane == 0, at, CZ - 1 - at) < 4
    group = RX // 8
    for x in range(group):
        packed = strips[1 - lane, x]
        for field, beside in enumerate((xsrc, xrden, xpold)):
            for k in range(8):
                lo = 16 * k + 4 * field
                moved = pltpu.roll(packed, lax.rem(256 - lo - 4 * lane, 128), 1)
                beside[k * group + x] = jnp.where(keep, moved, 0.0)
    source, scale = (esrc, xsrc), (erden, xrden)
    even, odd = (even0, even1), (odd0, odd1)
    sweep((epold, xpold), even, source, scale)
    sweep(even, odd, source, scale)
    sweep(odd, even, source, scale)

    def write(x, value):
        pressure[x] = value

    last_sweep(even, source, scale, write)
    slots = slot[...].astype(i32)
    values = forces_at(pressure[...].reshape(CX * CY, CZ), cell[...], nrm)
    values += [coords[c : c + 1, :] for c in range(3)]
    values += [disp[c : c + 1, :] for c in range(3)]
    values += [nrm[c : c + 1, :] for c in range(3)]
    values += [jnp.ones((1, PTS), f32)]
    sending[...] = to_slots(values, slots)


def second_fluid_kernel(
    place, erden, xrden, before, arrived, meta, strips, cell, nrm, slot,
    pressure_far, sending, src0, src1, even0, even1, odd0, odd1, pressure, sem,
):
    sub, lane = place[0], place[1]
    scale = (erden, xrden)
    for tile, (source, now) in enumerate(((src0, even0), (src1, even1))):
        cells = meta[...] if tile == 0 else strips[1 - lane, RX // 8]
        other = lane if tile == 0 else 1 - lane
        beside_x = jnp.zeros((8 * CY, CZ), f32)
        beside_y = jnp.zeros((CX * 8, CZ), f32)
        corner = jnp.zeros((64, CZ), f32)
        for dy, off_y in enumerate((0, 1, -1)):
            wanted = sub + off_y
            inside = (wanted >= 0) & (wanted < SUB)
            block = arrived[lax.rem(wanted + SUB, SUB) * LANE + other]
            block = jnp.where(inside, block, 0.0)
            for dx in range(3):
                values = joined(block[2 * dx : 2 * dx + 2])
                at = (dx * 3 + dy) * 2
                points = joined(cells[at : at + 2]).astype(i32)
                x, y, z = points >> 11, (points >> 7) & 15, points & 127
                if dx == 1:
                    x = jnp.where(x < 3, x, -1000)
                elif dx == 2:
                    x = jnp.where(x >= CX - 3, x - (CX - 8), -1000)
                if dy == 1:
                    y = jnp.where(y < 3, y, -1000000)
                elif dy == 2:
                    y = jnp.where(y >= CY - 3, y - (CY - 8), -1000000)
                edge = None if tile == 0 else lane
                if dx == 0 and dy == 0:
                    middle = spread(as_ones(ones_at(CX * CY, points >> 7)), z, values, edge)
                elif dy == 0:
                    beside_x = beside_x + spread(as_ones(ones_at(8 * CY, x * CY + y)), z, values, edge)
                elif dx == 0:
                    beside_y = beside_y + spread(as_ones(ones_at(CX * 8, x * 8 + y)), z, values, edge)
                else:
                    corner = corner + spread(as_ones(ones_at(64, x * 8 + y)), z, values, edge)
        for xs, ys, part in (
            (slice(0, CX), slice(0, CY), middle.reshape(CX, CY, CZ)),
            (slice(CX, RX), slice(0, CY), beside_x.reshape(8, CY, CZ)),
            (slice(0, CX), slice(CY, RY), beside_y.reshape(CX, 8, CZ)),
            (slice(CX, RX), slice(CY, RY), corner.reshape(8, 8, CZ)),
        ):
            source[xs, ys, :] = part
            now[xs, ys, :] = part * scale[tile][xs, ys, :]
    source, even, odd = (src0, src1), (even0, even1), (odd0, odd1)
    sweep(even, odd, source, scale)
    sweep(odd, even, source, scale)

    def write(x, value):
        pressure[x] = before[x] + value

    last_sweep(even, source, scale, write)
    copy = pltpu.make_async_copy(pressure, pressure_far, sem)
    copy.start()
    sending[...] = to_slots(forces_at(pressure[...].reshape(CX * CY, CZ), cell[...], nrm), slot[...].astype(i32))
    copy.wait()


def to_slots(values, slots):
    rank = slots & 7
    filler = [jnp.zeros((1, PTS), f32)] * (WIDE - len(values))
    block = jnp.concatenate(list(values) + filler, axis=0)
    stacked = jnp.concatenate([jnp.where(rank == r, block, 0.0) for r in range(CAP)], axis=0)
    owner = as_ones(ones_at(DOM, slots >> 3))
    total = None
    for part in pieces(stacked, 3):
        term = mxu(owner, part, NT)
        total = term if total is None else total + term
    return total


def from_slots(arrived, slots):
    rank = slots & 7
    owner = as_ones(ones_at(DOM, slots >> 3))
    flat = arrived.T
    total = None
    for part in pieces(flat, 3):
        term = mxu(part, owner, NN)
        total = term if total is None else total + term
    found = jnp.zeros((WIDE, PTS), f32)
    for r in range(CAP):
        found = found + jnp.where(rank == r, total[r * WIDE : (r + 1) * WIDE], 0.0)
    return found


def by_slot(received):
    flat = received.T
    return jnp.concatenate([flat[r * WIDE : (r + 1) * WIDE] for r in range(CAP)], axis=1)


def by_row(values):
    flat = jnp.concatenate([values[:, r * DOM : (r + 1) * DOM] for r in range(CAP)], axis=0)
    return flat.T


def product(left, head, tail, dims):
    a, b = pieces(left, 2)
    rows = left.shape[0]
    both = mxu(jnp.concatenate([a, b], axis=0), head, dims)
    return both[:rows] + both[rows:] + mxu(a, tail, dims)


def mapped_back(forces, khead, ktail, shell):
    loading = product(forces, khead, ktail, NN) * (1.0 / math.sqrt(PTS))
    shead, stail = pieces(shell, 2)
    displaced = loading + product(loading, shead, stail, NN)
    return product(displaced, khead, ktail, NT) * (1.0 / math.sqrt(NS))


def first_structure_kernel(received, nodes, shell, returned, mapped, khead, ktail):
    for r in range(CAP):
        distance = None
        for c in range(3):
            lane = r * WIDE + 3 + c
            gap = received[:, lane : lane + 1] - nodes[c : c + 1, :]
            distance = gap * gap if distance is None else distance + gap * gap
        weight = jnp.exp(-distance * inv_radius_sq)
        head, tail = pieces(weight, 2)
        khead[r * DOM : (r + 1) * DOM, :] = head
        ktail[r * DOM : (r + 1) * DOM, :] = tail
    held = by_slot(received[...])
    back = mapped_back(held[0:WIDE], khead[...], ktail[...], shell[...])
    mapped[...] = back
    moved = (source_gain * relaxation) * jnp.sum(held[9:12] * (back[0:3] - held[6:9]), axis=0, keepdims=True)
    rows = jnp.concatenate([moved, jnp.zeros((WIDE - 1, NS), f32)], axis=0)
    own = by_row(rows)
    at = lax.broadcasted_iota(i32, own.shape, 0)
    above = jnp.where(at == DOM - 1, 0.0, pltpu.roll(own, DOM - 1, 0))
    below = jnp.where(at == 0, 0.0, pltpu.roll(own, 1, 0))
    returned[...] = own + pltpu.roll(above, 1, 1) + pltpu.roll(below, 2, 1)


def second_structure_kernel(received, before, mapped, khead, ktail, shell, returned):
    forces = by_slot(received[...])
    held = by_slot(before[...])
    back = mapped_back(forces, khead[...], ktail[...], shell[...])
    t0, t1, d0, used = mapped[0:3, :], back[0:3], held[6:9], held[12:13]
    r0 = t0 - d0
    r1 = t1 - (d0 + relaxation * r0)
    delta = r1 - r0
    sums = []
    for term in (delta * r1, delta * delta, r1 * r1):
        inner = jnp.sum(term * used, axis=0, keepdims=True)
        sums.append(jnp.broadcast_to(jnp.sum(inner, axis=1, keepdims=True), (1, NS)))
    rows = jnp.concatenate([t1, t0, *sums, jnp.zeros((WIDE - 9, NS), f32)], axis=0)
    returned[...] = by_row(rows)


def hand_out_kernel(arrived, slot, high, low, out):
    held = arrived[...]
    rows = []
    for block in range(3):
        if block == 0:
            slots = slot[...]
        else:
            slots = joined((high if block == 1 else low)[10 * RY + 6 : 10 * RY + 8])
        found = from_slots(held, slots.astype(i32))
        rows += halves(found[block : block + 1])
    rows += [jnp.zeros((2, 128), f32)]
    payload = jnp.concatenate(rows, axis=0)
    for k in range(SUB * LANE):
        out[k] = payload


def arrive_kernel(arrived, slot, found, out):
    held = arrived[...]
    found[...] = from_slots(held, slot[...].astype(i32))
    total = jnp.sum(held, axis=0, keepdims=True)
    for k in range(SUB * LANE):
        out[k : k + 1, :] = total


def finish_kernel(found, sums, disp, rms):
    total = jnp.sum(sums[...], axis=0, keepdims=True)
    vr, vv, rr = total[:, 6:7], total[:, 7:8], total[:, 8:9]
    t1, t0 = found[0:3, :], found[3:6, :]
    disp[...] = t1 - (vr / (vv + epsilon)) * (t1 - t0)
    count = 3.0 * PTS * DOM * SUB * LANE
    rms[...] = jnp.sqrt(rr / count)


def shape(*dims, dtype=f32):
    return jax.ShapeDtypeStruct(dims, dtype)


def call(kernel, outs, args, scratch=(), scalars=0, name=None, far=(), far_out=()):
    def spec(k):
        space = pltpu.SMEM if k < scalars else pltpu.HBM if k in far else pltpu.VMEM
        return pl.BlockSpec(memory_space=space)

    return pl.pallas_call(
        kernel,
        out_shape=outs,
        in_specs=[spec(k) for k in range(len(args))],
        out_specs=tuple(
            pl.BlockSpec(memory_space=pltpu.HBM if k in far_out else pltpu.VMEM) for k in range(len(outs))
        ),
        scratch_shapes=list(scratch),
        compiler_params=pltpu.CompilerParams(vmem_limit_bytes=40 * 1024 * 1024),
        name=name,
    )(*args)


def body(rhs, coef, pold, cell_index, nrm, coords, partner, nodes, shell, disp):
    place = jnp.stack([lax.axis_index("sub"), lax.axis_index("lane")]).astype(i32)
    cell = cell_index.reshape(1, PTS)
    part = partner.reshape(1, PTS)
    block, half = shape(CX, CY, CZ), shape(RX, RY, CZ)
    row = shape(DOM, CAP * WIDE)

    def pair(low, high, axis):
        count = lax.axis_size(axis)
        fromhigh = lax.ppermute(low, axis, [(i + 1, i) for i in range(count - 1)])
        fromlow = lax.ppermute(high, axis, [(i, i + 1) for i in range(count - 1)])
        return fromhigh, fromlow

    def across(rows):
        return lax.all_to_all(rows, "dom", 0, 0, tiled=True)

    face, slab = shape(10 * CX + 8, CZ), shape(10 * RY + 8, CZ)
    src, rden, pold, low, high, slot, cell, nrm, disp = call(
        start_kernel,
        (block, block, block, face, face, shape(1, PTS), shape(1, PTS, dtype=i32), shape(3, PTS), shape(3, PTS)),
        (rhs, coef, pold, cell, part, nrm, disp),
        [pltpu.VMEM((CX, CY, CZ), f32)] * 2 + [pltpu.VMEM((1, PTS), i32), pltpu.SemaphoreType.DMA((7,))],
        name="start",
        far=range(7),
    )
    subhigh, sublow = pair(low, high, "sub")
    low, high = call(dom_kernel, (slab, slab), (src, rden, pold, cell, slot, subhigh, sublow), name="dom_slabs")
    domhigh, domlow = pair(low, high, "dom")
    esrc, erden, epold, strips, meta = call(
        lane_kernel,
        (half, half, half, shape(RX // 8 + 1, RY, CZ), shape(RY, CZ)),
        (place, src, rden, pold, cell, subhigh, sublow, domhigh, domlow),
        scalars=1,
        name="lane_strips",
    )
    strips = lax.all_gather(strips, "lane")
    grid = pltpu.VMEM((RX, RY, CZ), f32)
    pressure, xrden, sending = call(
        first_fluid_kernel,
        (block, half, row),
        (place, esrc, erden, epold, strips, cell, nrm, coords, disp, slot),
        [grid] * 6,
        scalars=1,
        name="first_fluid",
    )
    received = across(sending)
    square = shape(NS, NS, dtype=bf16)
    returned, mapped, khead, ktail = call(
        first_structure_kernel, (row, shape(WIDE, NS), square, square), (received, nodes, shell), name="first_structure"
    )
    arrived = across(returned)
    (spread_out,) = call(
        hand_out_kernel, (shape(SUB * LANE, 8, 128),), (arrived, slot, domhigh, domlow), name="hand_out"
    )
    values = lax.all_to_all(spread_out, ("sub", "lane"), 0, 0, tiled=True)
    pressure, sending = call(
        second_fluid_kernel,
        (block, row),
        (place, erden, xrden, pressure, values, meta, strips, cell, nrm, slot),
        [grid] * 6 + [pltpu.VMEM((CX, CY, CZ), f32), pltpu.SemaphoreType.DMA],
        scalars=1,
        name="second_fluid",
        far_out=(0,),
    )
    again = across(sending)
    (returned,) = call(
        second_structure_kernel, (row,), (again, received, mapped, khead, ktail, shell), name="second_structure"
    )
    arrived = across(returned)
    found, sums = call(
        arrive_kernel, (shape(WIDE, PTS), shape(SUB * LANE, 128)), (arrived, slot), name="arrive"
    )
    sums = lax.all_to_all(sums, ("sub", "lane"), 0, 0, tiled=True)
    disp_new, rms = call(finish_kernel, (shape(3, PTS), shape(1, 1)), (found, sums), name="finish")
    return pressure, disp_new, rms.reshape(())


def solution(mesh):
    every = ("dom", "sub", "lane")
    grid, points = P(*every), P(None, every)
    return jax.shard_map(
        body,
        mesh=mesh,
        in_specs=(grid, grid, grid, P(every), points, points, P(every, None), points, P(every, None), points),
        out_specs=(grid, points, P()),
        check_vma=False,
    )
```

```python
import math

import jax
import jax.numpy as jnp
from jax import lax
from jax.experimental import pallas as pl
from jax.experimental.pallas import tpu as pltpu
from jax.sharding import PartitionSpec as P

SWEEPS = 4
DOM, SUB, LANE = 64, 8, 2
CX, CY, CZ = 32, 16, 128
PTS, NS, CAP = 256, 512, 8
RX, RY = CX + 8, CY + 8
WIDE = 16

source_gain = 16.0
relaxation = 0.5
inv_radius_sq = 11.111111
epsilon = 1e-06

f32, bf16, i32 = jnp.float32, jnp.bfloat16, jnp.int32
NN = (((1,), (0,)), ((), ()))
NT = (((1,), (1,)), ((), ()))


def pieces(x, count):
    parts = []
    for _ in range(count - 1):
        head = x.astype(bf16)
        parts.append(head)
        x = x - head.astype(f32)
    parts.append(x.astype(bf16))
    return parts


def mxu(a, b, dims):
    return lax.dot_general(a, b, dims, preferred_element_type=f32)


def ones_at(rows, index):
    at = lax.broadcasted_iota(i32, (rows, index.shape[1]), 0)
    return at == index


def as_ones(mask):
    return jnp.where(mask, 1.0, 0.0).astype(bf16)


def spread(rows, z, values, edge=None):
    if edge is None:
        parts = pieces(jnp.where(ones_at(CZ, z), values, 0.0), 2)
    else:
        beside = jnp.where(edge == 0, z, z - (CZ - 16))
        parts = []
        for part in pieces(jnp.where(ones_at(16, beside), values, 0.0), 2):
            zero = jnp.zeros_like(part)
            first, last = jnp.where(edge == 0, part, zero), jnp.where(edge == 0, zero, part)
            parts.append(jnp.concatenate([first, jnp.zeros((CZ - 32, PTS), bf16), last], axis=0))
    total = None
    for part in parts:
        term = mxu(rows, part, NT)
        total = term if total is None else total + term
    return total


def halves(row):
    return row[:, 0:128], row[:, 128:256]


def joined(ref_rows):
    return jnp.concatenate([ref_rows[0:1], ref_rows[1:2]], axis=1)


def start_kernel(
    rhs_far, coef_far, pold_far, cell_far, part_far, nrm_far, disp_far,
    src, rden, pold, low, high, slot, cell, nrm, disp, rhs, coef, part, sems,
):
    pairs = (
        (cell_far, cell), (part_far, part), (nrm_far, nrm), (disp_far, disp),
        (rhs_far, rhs), (pold_far, pold), (coef_far, coef),
    )
    copies = [pltpu.make_async_copy(a, b, sems.at[k]) for k, (a, b) in enumerate(pairs)]
    for copy in copies:
        copy.start()
    for copy in copies[:4]:
        copy.wait()
    points = cell[...]
    values = source_gain * jnp.sum(disp[...] * nrm[...], axis=0, keepdims=True)
    added = spread(as_ones(ones_at(CX * CY, points >> 7)), points & 127, values)
    owner = ones_at(DOM, part[...])
    earlier = lax.broadcasted_iota(i32, (PTS, PTS), 0) < lax.broadcasted_iota(i32, (PTS, PTS), 1)
    before = mxu(as_ones(owner), as_ones(earlier), NN)
    rank = jnp.sum(jnp.where(owner, before, 0.0), axis=0, keepdims=True)
    slot[...] = part[...].astype(f32) * CAP + rank
    copies[4].wait()
    src[...] = rhs[...] + added.reshape(CX, CY, CZ)
    copies[6].wait()
    rden[...] = 1.0 / (6.0 + coef[...])
    copies[5].wait()
    tail = jnp.concatenate([*halves(points.astype(f32)), jnp.zeros((6, CZ), f32)], axis=0)
    for out, base3, base4 in ((low, 0, 0), (high, CY - 3, CY - 4)):
        for field, own, width, base in ((0, src, 3, base3), (3, rden, 3, base3), (6, pold, 4, base4)):
            for k in range(width):
                at = (field + k) * CX
                out[at : at + CX, :] = own[:, base + k, :]
        out[10 * CX : 10 * CX + 8, :] = tail


def dom_kernel(src, rden, pold, cell, slot, subhigh, sublow, low, high):
    tail = jnp.concatenate(
        [
            *halves(cell[...].astype(f32)),
            subhigh[10 * CX : 10 * CX + 2],
            sublow[10 * CX : 10 * CX + 2],
            *halves(slot[...]),
        ],
        axis=0,
    )
    for out, base3, base4 in ((low, 0, 0), (high, CX - 3, CX - 4)):
        for field, own, width, base in ((0, src, 3, base3), (3, rden, 3, base3), (6, pold, 4, base4)):
            for k in range(width):
                x, at = base + k, (field + k) * RY
                out[at : at + CY, :] = own[x]
                rows = [subhigh[(field + j) * CX + x : (field + j) * CX + x + 1] for j in range(width)]
                rows += [jnp.zeros((1, CZ), f32)] * (8 - 2 * width)
                rows += [sublow[(field + j) * CX + x : (field + j) * CX + x + 1] for j in range(width)]
                out[at + CY : at + RY, :] = jnp.concatenate(rows, axis=0)
        out[10 * RY : 10 * RY + 8, :] = tail


def lane_kernel(place, src, rden, pold, cell, subhigh, sublow, domhigh, domlow, esrc, erden, epold, strips, meta):
    for field, own, width, ext in ((0, src, 3, esrc), (3, rden, 3, erden), (6, pold, 4, epold)):
        ext[0:CX, 0:CY, :] = own[...]
        if width == 3:
            ext[0:CX, CY:RY, :] = jnp.zeros((CX, 8, CZ), f32)
            ext[CX + 3 : CX + 5] = jnp.zeros((2, RY, CZ), f32)
        for k in range(width):
            at = (field + k) * CX
            ext[0:CX, CY + k, :] = subhigh[at : at + CX]
            ext[0:CX, RY - width + k, :] = sublow[at : at + CX]
            at = (field + k) * RY
            ext[CX + k] = domhigh[at : at + RY]
            ext[RX - width + k] = domlow[at : at + RY]
    lane = place[1]
    shift = jnp.where(lane == 0, 4, 0)
    at = lax.broadcasted_iota(i32, (RY, CZ), 1)
    group = RX // 8
    for x in range(group):
        total = jnp.zeros((RY, CZ), f32)
        for k in range(8):
            for field, ext in enumerate((esrc, erden, epold)):
                lo = 16 * k + 4 * field
                moved = pltpu.roll(ext[k * group + x], lax.rem(lo + shift, 128), 1)
                total = jnp.where((at >= lo) & (at < lo + 4), moved, total)
        strips[x] = total
    a, b = halves(cell[...].astype(f32))
    cells = [a, b, subhigh[10 * CX : 10 * CX + 2], sublow[10 * CX : 10 * CX + 2]]
    cells += [domhigh[10 * RY : 10 * RY + 6], domlow[10 * RY : 10 * RY + 6], jnp.zeros((6, CZ), f32)]
    cells = jnp.concatenate(cells, axis=0)
    meta[...] = cells
    strips[group] = cells


def near(width):
    return [*range(CX + width), *range(RX - width, RX)]


def both(pair, x):
    return jnp.concatenate([pair[0][x], pair[1][x]], axis=1)


def sweep(now, out, source, scale, width):
    for x in near(width):
        here = both(now, x)
        total = both(now, (x + 1) % RX) + both(now, (x - 1) % RX)
        total = total + (pltpu.roll(here, RY - 1, 0) + pltpu.roll(here, 1, 0))
        total = total + (pltpu.roll(here, 2 * CZ - 1, 1) + pltpu.roll(here, 1, 1))
        total = (both(source, x) + total) * both(scale, x)
        out[0][x], out[1][x] = total[:, 0:CZ], total[:, CZ : 2 * CZ]


def last_sweep(now, source, scale, write):
    for x in range(CX):
        here = now[0][x]
        total = now[0][(x + 1) % RX, 0:CY] + now[0][(x - 1) % RX, 0:CY]
        total = total + (pltpu.roll(here, RY - 1, 0) + pltpu.roll(here, 1, 0))[0:CY]
        wide = jnp.concatenate([here[0:CY], now[1][x, 0:CY]], axis=1)
        beside = pltpu.roll(wide, 2 * CZ - 1, 1) + pltpu.roll(wide, 1, 1)
        write(x, (source[0][x, 0:CY] + (total + beside[:, 0:CZ])) * scale[0][x, 0:CY])


def forces_at(pressure, points, nrm):
    at_z = as_ones(ones_at(CZ, points & 127))
    total = None
    for part in pieces(pressure, 2):
        term = mxu(part, at_z, NN)
        total = term if total is None else total + term
    press = jnp.sum(jnp.where(ones_at(CX * CY, points >> 7), total, 0.0), axis=0, keepdims=True)
    return [press * nrm[c : c + 1, :] for c in range(3)]


def first_fluid_kernel(
    place, esrc, erden, epold, strips, cell, nrm, coords, disp, slot,
    pressure, xrden, sending, xsrc, xpold, even0, even1, odd0, odd1,
):
    lane = place[1]
    at = lax.broadcasted_iota(i32, (RY, CZ), 1)
    keep = jnp.where(lane == 0, at, CZ - 1 - at) < 4
    group = RX // 8
    for x in range(group):
        packed = strips[1 - lane, x]
        for field, beside in enumerate((xsrc, xrden, xpold)):
            for k in range(8):
                lo = 16 * k + 4 * field
                moved = pltpu.roll(packed, lax.rem(256 - lo - 4 * lane, 128), 1)
                beside[k * group + x] = jnp.where(keep, moved, 0.0)
    source, scale = (esrc, xsrc), (erden, xrden)
    even, odd = (even0, even1), (odd0, odd1)
    sweep((epold, xpold), even, source, scale, 3)
    sweep(even, odd, source, scale, 2)
    sweep(odd, even, source, scale, 1)

    def write(x, value):
        pressure[x] = value

    last_sweep(even, source, scale, write)
    slots = slot[...].astype(i32)
    values = forces_at(pressure[...].reshape(CX * CY, CZ), cell[...], nrm)
    values += [coords[c : c + 1, :] for c in range(3)]
    values += [disp[c : c + 1, :] for c in range(3)]
    values += [nrm[c : c + 1, :] for c in range(3)]
    values += [jnp.ones((1, PTS), f32)]
    sending[...] = to_slots(values, slots, 3)


def second_fluid_kernel(
    place, erden, xrden, before, arrived, meta, strips, cell, nrm, slot,
    pressure_far, sending, src0, src1, even0, even1, odd0, odd1, pressure, sem,
):
    sub, lane = place[0], place[1]
    scale = (erden, xrden)
    for tile, (source, now) in enumerate(((src0, even0), (src1, even1))):
        cells = meta[...] if tile == 0 else strips[1 - lane, RX // 8]
        other = lane if tile == 0 else 1 - lane
        beside_x = jnp.zeros((8 * CY, CZ), f32)
        beside_y = jnp.zeros((CX * 8, CZ), f32)
        corner = jnp.zeros((64, CZ), f32)
        for dy, off_y in enumerate((0, 1, -1)):
            wanted = sub + off_y
            inside = (wanted >= 0) & (wanted < SUB)
            block = arrived[lax.rem(wanted + SUB, SUB) * LANE + other]
            block = jnp.where(inside, block, 0.0)
            for dx in range(3):
                values = joined(block[2 * dx : 2 * dx + 2])
                at = (dx * 3 + dy) * 2
                points = joined(cells[at : at + 2]).astype(i32)
                x, y, z = points >> 11, (points >> 7) & 15, points & 127
                if dx == 1:
                    x = jnp.where(x < 3, x, -1000)
                elif dx == 2:
                    x = jnp.where(x >= CX - 3, x - (CX - 8), -1000)
                if dy == 1:
                    y = jnp.where(y < 3, y, -1000000)
                elif dy == 2:
                    y = jnp.where(y >= CY - 3, y - (CY - 8), -1000000)
                edge = None if tile == 0 else lane
                if dx == 0 and dy == 0:
                    middle = spread(as_ones(ones_at(CX * CY, points >> 7)), z, values, edge)
                elif dy == 0:
                    beside_x = beside_x + spread(as_ones(ones_at(8 * CY, x * CY + y)), z, values, edge)
                elif dx == 0:
                    beside_y = beside_y + spread(as_ones(ones_at(CX * 8, x * 8 + y)), z, values, edge)
                else:
                    corner = corner + spread(as_ones(ones_at(64, x * 8 + y)), z, values, edge)
        for xs, ys, part in (
            (slice(0, CX), slice(0, CY), middle.reshape(CX, CY, CZ)),
            (slice(CX, RX), slice(0, CY), beside_x.reshape(8, CY, CZ)),
            (slice(0, CX), slice(CY, RY), beside_y.reshape(CX, 8, CZ)),
            (slice(CX, RX), slice(CY, RY), corner.reshape(8, 8, CZ)),
        ):
            source[xs, ys, :] = part
            now[xs, ys, :] = part * scale[tile][xs, ys, :]
    source, even, odd = (src0, src1), (even0, even1), (odd0, odd1)
    sweep(even, odd, source, scale, 2)
    sweep(odd, even, source, scale, 1)

    def write(x, value):
        pressure[x] = before[x] + value

    last_sweep(even, source, scale, write)
    copy = pltpu.make_async_copy(pressure, pressure_far, sem)
    copy.start()
    sending[...] = to_slots(forces_at(pressure[...].reshape(CX * CY, CZ), cell[...], nrm), slot[...].astype(i32), 2)
    copy.wait()


def to_slots(values, slots, count):
    rank = slots & 7
    filler = [jnp.zeros((1, PTS), f32)] * (WIDE - len(values))
    block = jnp.concatenate(list(values) + filler, axis=0)
    stacked = jnp.concatenate([jnp.where(rank == r, block, 0.0) for r in range(CAP)], axis=0)
    owner = as_ones(ones_at(DOM, slots >> 3))
    total = None
    for part in pieces(stacked, count):
        term = mxu(owner, part, NT)
        total = term if total is None else total + term
    return total


def from_slots(arrived, slots):
    rank = slots & 7
    owner = as_ones(ones_at(DOM, slots >> 3))
    flat = arrived.T
    total = None
    for part in pieces(flat, 2):
        term = mxu(part, owner, NN)
        total = term if total is None else total + term
    found = jnp.zeros((WIDE, PTS), f32)
    for r in range(CAP):
        found = found + jnp.where(rank == r, total[r * WIDE : (r + 1) * WIDE], 0.0)
    return found


def by_slot(received):
    flat = received.T
    return jnp.concatenate([flat[r * WIDE : (r + 1) * WIDE] for r in range(CAP)], axis=1)


def by_row(values):
    flat = jnp.concatenate([values[:, r * DOM : (r + 1) * DOM] for r in range(CAP)], axis=0)
    return flat.T


def product(left, head, tail, dims):
    a, b = pieces(left, 2)
    rows = left.shape[0]
    both = mxu(jnp.concatenate([a, b], axis=0), head, dims)
    return both[:rows] + both[rows:] + mxu(a, tail, dims)


def mapped_back(forces, khead, ktail, shell):
    loading = product(forces, khead, ktail, NN) * (1.0 / math.sqrt(PTS))
    shead, stail = pieces(shell, 2)
    displaced = loading + product(loading, shead, stail, NN)
    return product(displaced, khead, ktail, NT) * (1.0 / math.sqrt(NS))


def first_structure_kernel(received, nodes, shell, returned, mapped, khead, ktail):
    for r in range(CAP):
        distance = None
        for c in range(3):
            lane = r * WIDE + 3 + c
            gap = received[:, lane : lane + 1] - nodes[c : c + 1, :]
            distance = gap * gap if distance is None else distance + gap * gap
        weight = jnp.exp(-distance * inv_radius_sq)
        head, tail = pieces(weight, 2)
        khead[r * DOM : (r + 1) * DOM, :] = head
        ktail[r * DOM : (r + 1) * DOM, :] = tail
    held = by_slot(received[...])
    back = mapped_back(held[0:WIDE], khead[...], ktail[...], shell[...])
    mapped[...] = back
    moved = (source_gain * relaxation) * jnp.sum(held[9:12] * (back[0:3] - held[6:9]), axis=0, keepdims=True)
    rows = jnp.concatenate([moved, jnp.zeros((WIDE - 1, NS), f32)], axis=0)
    own = by_row(rows)
    at = lax.broadcasted_iota(i32, own.shape, 0)
    above = jnp.where(at == DOM - 1, 0.0, pltpu.roll(own, DOM - 1, 0))
    below = jnp.where(at == 0, 0.0, pltpu.roll(own, 1, 0))
    returned[...] = own + pltpu.roll(above, 1, 1) + pltpu.roll(below, 2, 1)


def second_structure_kernel(received, before, mapped, khead, ktail, shell, returned):
    forces = by_slot(received[...])
    held = by_slot(before[...])
    back = mapped_back(forces, khead[...], ktail[...], shell[...])
    t0, t1, d0, used = mapped[0:3, :], back[0:3], held[6:9], held[12:13]
    r0 = t0 - d0
    r1 = t1 - (d0 + relaxation * r0)
    delta = r1 - r0
    sums = []
    for term in (delta * r1, delta * delta, r1 * r1):
        inner = jnp.sum(term * used, axis=0, keepdims=True)
        sums.append(jnp.broadcast_to(jnp.sum(inner, axis=1, keepdims=True), (1, NS)))
    rows = jnp.concatenate([t1, t0, *sums, jnp.zeros((WIDE - 9, NS), f32)], axis=0)
    returned[...] = by_row(rows)


def hand_out_kernel(arrived, slot, high, low, out):
    held = arrived[...]
    rows = []
    for block in range(3):
        if block == 0:
            slots = slot[...]
        else:
            slots = joined((high if block == 1 else low)[10 * RY + 6 : 10 * RY + 8])
        found = from_slots(held, slots.astype(i32))
        rows += halves(found[block : block + 1])
    rows += [jnp.zeros((2, 128), f32)]
    payload = jnp.concatenate(rows, axis=0)
    for k in range(SUB * LANE):
        out[k] = payload


def arrive_kernel(arrived, slot, found, out):
    held = arrived[...]
    found[...] = from_slots(held, slot[...].astype(i32))
    total = jnp.sum(held, axis=0, keepdims=True)
    for k in range(SUB * LANE):
        out[k : k + 1, :] = total


def finish_kernel(found, sums, disp, rms):
    total = jnp.sum(sums[...], axis=0, keepdims=True)
    vr, vv, rr = total[:, 6:7], total[:, 7:8], total[:, 8:9]
    t1, t0 = found[0:3, :], found[3:6, :]
    disp[...] = t1 - (vr / (vv + epsilon)) * (t1 - t0)
    count = 3.0 * PTS * DOM * SUB * LANE
    rms[...] = jnp.sqrt(rr / count)


def shape(*dims, dtype=f32):
    return jax.ShapeDtypeStruct(dims, dtype)


def call(kernel, outs, args, scratch=(), scalars=0, name=None, far=(), far_out=()):
    def spec(k):
        space = pltpu.SMEM if k < scalars else pltpu.HBM if k in far else pltpu.VMEM
        return pl.BlockSpec(memory_space=space)

    return pl.pallas_call(
        kernel,
        out_shape=outs,
        in_specs=[spec(k) for k in range(len(args))],
        out_specs=tuple(
            pl.BlockSpec(memory_space=pltpu.HBM if k in far_out else pltpu.VMEM) for k in range(len(outs))
        ),
        scratch_shapes=list(scratch),
        compiler_params=pltpu.CompilerParams(vmem_limit_bytes=40 * 1024 * 1024),
        name=name,
    )(*args)


def body(rhs, coef, pold, cell_index, nrm, coords, partner, nodes, shell, disp):
    place = jnp.stack([lax.axis_index("sub"), lax.axis_index("lane")]).astype(i32)
    cell = cell_index.reshape(1, PTS)
    part = partner.reshape(1, PTS)
    block, half = shape(CX, CY, CZ), shape(RX, RY, CZ)
    row = shape(DOM, CAP * WIDE)

    def pair(low, high, axis):
        count = lax.axis_size(axis)
        fromhigh = lax.ppermute(low, axis, [(i + 1, i) for i in range(count - 1)])
        fromlow = lax.ppermute(high, axis, [(i, i + 1) for i in range(count - 1)])
        return fromhigh, fromlow

    def across(rows):
        return lax.all_to_all(rows, "dom", 0, 0, tiled=True)

    face, slab = shape(10 * CX + 8, CZ), shape(10 * RY + 8, CZ)
    src, rden, pold, low, high, slot, cell, nrm, disp = call(
        start_kernel,
        (block, block, block, face, face, shape(1, PTS), shape(1, PTS, dtype=i32), shape(3, PTS), shape(3, PTS)),
        [pltpu.with_memory_space_constraint(x, pltpu.HBM) for x in (rhs, coef, pold, cell, part, nrm, disp)],
        [pltpu.VMEM((CX, CY, CZ), f32)] * 2 + [pltpu.VMEM((1, PTS), i32), pltpu.SemaphoreType.DMA((7,))],
        name="start",
        far=range(7),
    )
    subhigh, sublow = pair(low, high, "sub")
    low, high = call(dom_kernel, (slab, slab), (src, rden, pold, cell, slot, subhigh, sublow), name="dom_slabs")
    domhigh, domlow = pair(low, high, "dom")
    esrc, erden, epold, strips, meta = call(
        lane_kernel,
        (half, half, half, shape(RX // 8 + 1, RY, CZ), shape(RY, CZ)),
        (place, src, rden, pold, cell, subhigh, sublow, domhigh, domlow),
        scalars=1,
        name="lane_strips",
    )
    strips = lax.all_gather(strips, "lane")
    grid = pltpu.VMEM((RX, RY, CZ), f32)
    pressure, xrden, sending = call(
        first_fluid_kernel,
        (block, half, row),
        (place, esrc, erden, epold, strips, cell, nrm, coords, disp, slot),
        [grid] * 6,
        scalars=1,
        name="first_fluid",
    )
    received = across(sending)
    square = shape(NS, NS, dtype=bf16)
    returned, mapped, khead, ktail = call(
        first_structure_kernel, (row, shape(WIDE, NS), square, square), (received, nodes, shell), name="first_structure"
    )
    arrived = across(returned)
    (spread_out,) = call(
        hand_out_kernel, (shape(SUB * LANE, 8, 128),), (arrived, slot, domhigh, domlow), name="hand_out"
    )
    values = lax.all_to_all(spread_out, ("sub", "lane"), 0, 0, tiled=True)
    pressure, sending = call(
        second_fluid_kernel,
        (block, row),
        (place, erden, xrden, pressure, values, meta, strips, cell, nrm, slot),
        [grid] * 6 + [pltpu.VMEM((CX, CY, CZ), f32), pltpu.SemaphoreType.DMA],
        scalars=1,
        name="second_fluid",
        far_out=(0,),
    )
    again = across(sending)
    (returned,) = call(
        second_structure_kernel, (row,), (again, received, mapped, khead, ktail, shell), name="second_structure"
    )
    arrived = across(returned)
    found, sums = call(
        arrive_kernel, (shape(WIDE, PTS), shape(SUB * LANE, 128)), (arrived, slot), name="arrive"
    )
    sums = lax.all_to_all(sums, ("sub", "lane"), 0, 0, tiled=True)
    disp_new, rms = call(finish_kernel, (shape(3, PTS), shape(1, 1)), (found, sums), name="finish")
    return pressure, disp_new, rms.reshape(())


def solution(mesh):
    every = ("dom", "sub", "lane")
    grid, points = P(*every), P(None, every)
    return jax.shard_map(
        body,
        mesh=mesh,
        in_specs=(grid, grid, grid, P(every), points, points, P(every, None), points, P(every, None), points),
        out_specs=(grid, points, P()),
        check_vma=False,
    )
```

```python
import math

import jax
import jax.numpy as jnp
from jax import lax
from jax.experimental import pallas as pl
from jax.experimental.pallas import tpu as pltpu
from jax.sharding import PartitionSpec as P

SWEEPS = 4
DOM, SUB, LANE = 64, 8, 2
CX, CY, CZ = 32, 16, 128
PTS, NS, CAP = 256, 512, 8
RX, RY = CX + 8, CY + 8
WIDE = 16
FACE, SLAB = 10 * CX, 10 * RY

source_gain = 16.0
relaxation = 0.5
inv_radius_sq = 11.111111
epsilon = 1e-06

f32, bf16, i32 = jnp.float32, jnp.bfloat16, jnp.int32
NN = (((1,), (0,)), ((), ()))
NT = (((1,), (1,)), ((), ()))


def pieces(x, count):
    parts = []
    for _ in range(count - 1):
        head = x.astype(bf16)
        parts.append(head)
        x = x - head.astype(f32)
    parts.append(x.astype(bf16))
    return parts


def mxu(a, b, dims):
    return lax.dot_general(a, b, dims, preferred_element_type=f32)


def ones_at(rows, index):
    at = lax.broadcasted_iota(i32, (rows, index.shape[1]), 0)
    return at == index


def as_ones(mask):
    return jnp.where(mask, 1.0, 0.0).astype(bf16)


def spread(rows, z, values, edge=None):
    if edge is None:
        parts = pieces(jnp.where(ones_at(CZ, z), values, 0.0), 2)
    else:
        beside = jnp.where(edge == 0, z, z - (CZ - 16))
        parts = []
        for part in pieces(jnp.where(ones_at(16, beside), values, 0.0), 2):
            zero = jnp.zeros_like(part)
            first, last = jnp.where(edge == 0, part, zero), jnp.where(edge == 0, zero, part)
            parts.append(jnp.concatenate([first, jnp.zeros((CZ - 32, PTS), bf16), last], axis=0))
    total = None
    for part in parts:
        term = mxu(rows, part, NT)
        total = term if total is None else total + term
    return total


def halves(row):
    return row[:, 0:128], row[:, 128:256]


def joined(ref_rows):
    return jnp.concatenate([ref_rows[0:1], ref_rows[1:2]], axis=1)


def up_down(core, beside, across):
    return jnp.where(core == 0, beside, across), jnp.where(core == 0, across, beside)


def start_kernel(
    rhs_far, coef_far, pold_far, cell_far, part_far, nrm_far, disp_far, coords_far,
    src, rden, pold, strips, slot, cell, nrm, disp, coords, rhs, coef, part, sems,
):
    pairs = (
        (cell_far, cell), (part_far, part), (nrm_far, nrm), (disp_far, disp),
        (rhs_far, rhs), (pold_far, pold), (coef_far, coef), (coords_far, coords),
    )
    copies = [pltpu.make_async_copy(a, b, sems.at[k]) for k, (a, b) in enumerate(pairs)]
    for copy in copies:
        copy.start()
    for copy in copies[:4]:
        copy.wait()
    points = cell[...]
    values = source_gain * jnp.sum(disp[...] * nrm[...], axis=0, keepdims=True)
    added = spread(as_ones(ones_at(CX * CY, points >> 7)), points & 127, values)
    owner = ones_at(DOM, part[...])
    earlier = lax.broadcasted_iota(i32, (PTS, PTS), 0) < lax.broadcasted_iota(i32, (PTS, PTS), 1)
    before = mxu(as_ones(owner), as_ones(earlier), NN)
    rank = jnp.sum(jnp.where(owner, before, 0.0), axis=0, keepdims=True)
    slot[...] = part[...].astype(f32) * CAP + rank
    copies[4].wait()
    src[...] = rhs[...] + added.reshape(CX, CY, CZ)
    copies[6].wait()
    rden[...] = 1.0 / (6.0 + coef[...])
    copies[5].wait()
    copies[7].wait()
    shift = jnp.where(lax.axis_index("lane") == 0, 4, 0)
    at = lax.broadcasted_iota(i32, (CY, CZ), 1)
    for x4 in range(4):
        strips[x4 * CY : (x4 + 1) * CY, :] = packed([lambda k, f=f: f[4 * k + x4] for f in (src, rden, pold)], at, shift)
    tail = [*halves(points.astype(f32)), *halves(slot[...]), jnp.zeros((4, CZ), f32)]
    strips[64:72, :] = jnp.concatenate(tail, axis=0)


def packed(fields, at, shift):
    total = jnp.zeros(at.shape, f32)
    for k in range(8):
        for number, field in enumerate(fields):
            lo = 16 * k + 4 * number
            total = jnp.where((at >= lo) & (at < lo + 4), pltpu.roll(field(k), lax.rem(lo + shift, 128), 1), total)
    return total


def unpacked(rows, lo, lane, keep):
    return jnp.where(keep, pltpu.roll(rows, lax.rem(256 - lo - 4 * lane, 128), 1), 0.0)


def edges(lane, rows):
    at = lax.broadcasted_iota(i32, (rows, CZ), 1)
    return jnp.where(lane == 0, at, CZ - 1 - at) < 4


def faces_kernel(src, rden, pold, cell, lanes, across, beside):
    core, lane = lax.rem(lax.axis_index("sub"), 2), lax.axis_index("lane")
    for field, own, width in ((0, src, 3), (3, rden, 3), (6, pold, 4)):
        for k in range(width):
            at = (field + k) * CX
            low, high = own[:, k, :], own[:, CY - width + k, :]
            beside[at : at + CX, :], across[at : at + CX, :] = up_down(core, high, low)
    other = lanes[1 - lane]
    for x4 in range(4):
        at, low, high = FACE + 4 * x4, other[x4 * CY : x4 * CY + 4], other[(x4 + 1) * CY - 4 : (x4 + 1) * CY]
        beside[at : at + 4, :], across[at : at + 4, :] = up_down(core, high, low)
    tail = jnp.concatenate([*halves(cell[...].astype(f32)), other[64:66], jnp.zeros((4, CZ), f32)], axis=0)
    beside[FACE + 16 : FACE + 24, :] = tail
    across[FACE + 16 : FACE + 24, :] = tail


def dom_kernel(
    src, rden, pold, cell, slot, fromacross, cores, lanes, beside, across, subhigh, sublow, beyond, tails, slabs
):
    core, lane = lax.rem(lax.axis_index("sub"), 2), lax.axis_index("lane")
    subhigh[...], sublow[...] = up_down(core, cores[1 - core], fromacross[...])
    other = lanes[1 - lane]
    cellhigh, celllow = subhigh[FACE + 16 : FACE + 24], sublow[FACE + 16 : FACE + 24]
    tail = [*halves(cell[...].astype(f32)), cellhigh[0:2], celllow[0:2], *halves(slot[...])]
    tails[0:8] = jnp.concatenate(tail, axis=0)
    tails[8:16] = jnp.concatenate([other[64:66], cellhigh[2:4], celllow[2:4], other[66:68]], axis=0)
    for x4 in range(4):
        at = FACE + 4 * x4
        sides = subhigh[at : at + 4], sublow[at : at + 4]
        beyond[x4] = jnp.concatenate([other[x4 * CY : (x4 + 1) * CY], *sides], axis=0)
    at = lax.broadcasted_iota(i32, (RY, CZ), 1)
    low, high = slabs.at[0], slabs.at[1]
    for out, base3, base4, group in ((low, 0, 0, 0), (high, CX - 3, CX - 4, 7)):
        for field, own, width, base in ((0, src, 3, base3), (3, rden, 3, base3), (6, pold, 4, base4)):
            for k in range(width):
                x, row = base + k, (field + k) * RY
                out[row : row + CY, :] = own[x]
                rows = [subhigh[(field + j) * CX + x : (field + j) * CX + x + 1] for j in range(width)]
                rows += [jnp.zeros((1, CZ), f32)] * (8 - 2 * width)
                rows += [sublow[(field + j) * CX + x : (field + j) * CX + x + 1] for j in range(width)]
                out[row + CY : row + RY, :] = jnp.concatenate(rows, axis=0)
        total = jnp.zeros((RY, CZ), f32)
        for j in range(4):
            moved = pltpu.roll(beyond[j], (16 * j - 16 * group) % 128, 1)
            total = jnp.where((at >= 16 * j) & (at < 16 * j + 16), moved, total)
        out[SLAB : SLAB + RY, :] = total
        out[SLAB + RY : SLAB + RY + 16, :] = tails[...]
    beside[...], across[...] = up_down(lax.rem(lax.axis_index("dom"), 2), high[...], low[...])


def ring_kernel(src, rden, pold, subhigh, sublow, beyond, esrc, erden, epold, xsrc, xrden, xpold):
    for field, own, width, ext in ((0, src, 3, esrc), (3, rden, 3, erden), (6, pold, 4, epold)):
        ext[:, 0:CY, :] = own[...]
        if width == 3:
            ext[:, CY:RY, :] = jnp.zeros((CX, 8, CZ), f32)
        for k in range(width):
            at = (field + k) * CX
            ext[:, CY + k, :] = subhigh[at : at + CX]
            ext[:, RY - width + k, :] = sublow[at : at + CX]
    lane = lax.axis_index("lane")
    keep = edges(lane, RY)
    for x4 in range(4):
        rows = beyond[x4]
        for field, beside in enumerate((xsrc, xrden, xpold)):
            for k in range(8):
                beside[4 * k + x4] = unpacked(rows, 16 * k + 4 * field, lane, keep)


def near(width):
    return [*range(CX + width), *range(RX - width, RX)]


def ring(own, other, own_halo=None, other_halo=None):
    def layer(x):
        if x < CX or own_halo is None:
            return jnp.concatenate([own[x], other[x]], axis=1)
        return jnp.concatenate([own_halo(x - CX), other_halo[x - CX]], axis=1)

    return layer


def sweep(now, out, source, scale, width):
    for x in near(width):
        here = now(x)
        total = now((x + 1) % RX) + now((x - 1) % RX)
        total = total + (pltpu.roll(here, RY - 1, 0) + pltpu.roll(here, 1, 0))
        total = total + (pltpu.roll(here, 2 * CZ - 1, 1) + pltpu.roll(here, 1, 1))
        total = (source(x) + total) * scale(x)
        out[0][x], out[1][x] = total[:, 0:CZ], total[:, CZ : 2 * CZ]


def last_sweep(now, source, scale, write):
    for x in range(CX):
        here = now[0][x]
        total = now[0][(x + 1) % RX, 0:CY] + now[0][(x - 1) % RX, 0:CY]
        total = total + (pltpu.roll(here, RY - 1, 0) + pltpu.roll(here, 1, 0))[0:CY]
        wide = jnp.concatenate([here[0:CY], now[1][x, 0:CY]], axis=1)
        beside = pltpu.roll(wide, 2 * CZ - 1, 1) + pltpu.roll(wide, 1, 1)
        write(x, (source[x, 0:CY] + (total + beside[:, 0:CZ])) * scale[x, 0:CY])


def forces_at(pressure, points, nrm):
    at_z = as_ones(ones_at(CZ, points & 127))
    total = None
    for part in pieces(pressure, 2):
        term = mxu(part, at_z, NN)
        total = term if total is None else total + term
    press = jnp.sum(jnp.where(ones_at(CX * CY, points >> 7), total, 0.0), axis=0, keepdims=True)
    return [press * nrm[c : c + 1, :] for c in range(3)]


def first_fluid_kernel(
    esrc, erden, epold, xsrc, xrden, xpold, doms, fromacross, tails, cell, nrm, coords, disp, slot,
    pressure, hrden0, hrden1, meta, sending, hsrc1, hpold1, domhigh, domlow, even0, even1, odd0, odd1,
):
    lane, pair = lax.axis_index("lane"), lax.rem(lax.axis_index("dom"), 2)
    domhigh[...], domlow[...] = up_down(pair, doms[1 - pair], fromacross[...])
    keep = edges(lane, RY)
    for base, slab in ((0, domhigh), (4, domlow)):
        rows = slab[SLAB : SLAB + RY]
        for j in range(4):
            for field, halo in enumerate((hsrc1, hrden1, hpold1)):
                halo[base + j] = unpacked(rows, 16 * j + 4 * field, lane, keep)

    def halo(field, width):
        def layer(x):
            slab, k = (domhigh, x) if x < 4 else (domlow, x - (8 - width))
            return slab[(field + k) * RY : (field + k + 1) * RY]

        return layer

    for x in range(8):
        hrden0[x] = jnp.zeros((RY, CZ), f32) if x in (3, 4) else halo(3, 3)(x)
    source = ring(esrc, xsrc, halo(0, 3), hsrc1)
    scale = ring(erden, xrden, halo(3, 3), hrden1)
    even, odd = (even0, even1), (odd0, odd1)
    sweep(ring(epold, xpold, halo(6, 4), hpold1), even, source, scale, 3)
    sweep(ring(*even), odd, source, scale, 2)
    sweep(ring(*odd), even, source, scale, 1)

    def write(x, value):
        pressure[x] = value

    last_sweep(even, esrc, erden, write)
    slots = slot[...].astype(i32)
    values = forces_at(pressure[...].reshape(CX * CY, CZ), cell[...], nrm)
    values += [coords[c : c + 1, :] for c in range(3)]
    values += [disp[c : c + 1, :] for c in range(3)]
    values += [nrm[c : c + 1, :] for c in range(3)]
    values += [jnp.ones((1, PTS), f32)]
    sending[...] = to_slots(values, slots, 3)
    for tile in range(2):
        own = tails[8 * tile : 8 * tile + 8]
        at = SLAB + RY + 8 * tile
        up, down = domhigh[at : at + 8], domlow[at : at + 8]
        meta[24 * tile : 24 * tile + 24] = jnp.concatenate([own[0:6], up[0:6], down[0:6], own[6:], up[6:], down[6:]], axis=0)


def placed(values, points, dx, dy, edge):
    x, y, z = points >> 11, (points >> 7) & 15, points & 127
    if dx == 1:
        x = jnp.where(x < 3, x, -1000)
    elif dx == 2:
        x = jnp.where(x >= CX - 3, x - (CX - 8), -1000)
    if dy == 1:
        y = jnp.where(y < 3, y, -1000000)
    elif dy == 2:
        y = jnp.where(y >= CY - 3, y - (CY - 8), -1000000)
    wide, deep = CY if dy == 0 else 8, CX if dx == 0 else 8
    return spread(as_ones(ones_at(deep * wide, x * wide + y)), z, values, edge).reshape(deep, wide, CZ)


def own_rows_kernel(values, meta, src0, src1):
    lane = lax.axis_index("lane")
    for tile, source in enumerate((src0, src1)):
        parts = []
        for dx in range(3):
            at, row = 6 * tile + 2 * dx, 24 * tile + 6 * dx
            points = joined(meta[row : row + 2]).astype(i32)
            parts.append(placed(joined(values[at : at + 2]), points, dx, 0, None if tile == 0 else lane))
        source[0:CX] = parts[0]
        source[CX:RX] = parts[1] + parts[2]


def second_fluid_kernel(
    erden, xrden, hrden0, hrden1, before, own0, own1, fromacross, cores, meta, cell, nrm, slot,
    pressure_far, sending, src0, src1, even0, even1, odd0, odd1, pressure, fromhigh, fromlow, sem,
):
    lane, core = lax.axis_index("lane"), lax.rem(lax.axis_index("sub"), 2)
    fromhigh[...], fromlow[...] = up_down(core, cores[1 - core], fromacross[...])
    for tile, (source, now, own, scale, halo) in enumerate(
        ((src0, even0, own0, erden, hrden0), (src1, even1, own1, xrden, hrden1))
    ):
        beside = [None] * 3
        for dy, values in ((1, fromhigh), (2, fromlow)):
            for dx in range(3):
                at, row = 6 * tile + 2 * dx, 24 * tile + 6 * dx + 2 * dy
                points = joined(meta[row : row + 2]).astype(i32)
                part = placed(joined(values[at : at + 2]), points, dx, dy, None if tile == 0 else lane)
                beside[dx] = part if dy == 1 else beside[dx] + part
        for ys, part in ((slice(0, CY), own[0:CX]), (slice(CY, RY), beside[0])):
            source[0:CX, ys, :] = part
            now[0:CX, ys, :] = part * scale[:, ys, :]
        for ys, part in ((slice(0, CY), own[CX:RX]), (slice(CY, RY), beside[1] + beside[2])):
            source[CX:RX, ys, :] = part
            now[CX:RX, ys, :] = part * halo[:, ys, :]
    even, odd = (even0, even1), (odd0, odd1)
    source = ring(src0, src1)
    scale = ring(erden, xrden, lambda x: hrden0[x], hrden1)
    sweep(ring(*even), odd, source, scale, 2)
    sweep(ring(*odd), even, source, scale, 1)

    def write(x, value):
        pressure[x] = before[x] + value

    last_sweep(even, src0, erden, write)
    copy = pltpu.make_async_copy(pressure, pressure_far, sem)
    copy.start()
    sending[...] = to_slots(forces_at(pressure[...].reshape(CX * CY, CZ), cell[...], nrm), slot[...].astype(i32), 2)
    copy.wait()


def to_slots(values, slots, count):
    rank = slots & 7
    filler = [jnp.zeros((1, PTS), f32)] * (WIDE - len(values))
    block = jnp.concatenate(list(values) + filler, axis=0)
    stacked = jnp.concatenate([jnp.where(rank == r, block, 0.0) for r in range(CAP)], axis=0)
    owner = as_ones(ones_at(DOM, slots >> 3))
    total = None
    for part in pieces(stacked, count):
        term = mxu(owner, part, NT)
        total = term if total is None else total + term
    return total


def from_slots(arrived, slots):
    rank = slots & 7
    owner = as_ones(ones_at(DOM, slots >> 3))
    flat = arrived.T
    total = None
    for part in pieces(flat, 2):
        term = mxu(part, owner, NN)
        total = term if total is None else total + term
    found = jnp.zeros((WIDE, PTS), f32)
    for r in range(CAP):
        found = found + jnp.where(rank == r, total[r * WIDE : (r + 1) * WIDE], 0.0)
    return found


def by_slot(received):
    flat = received.T
    return jnp.concatenate([flat[r * WIDE : (r + 1) * WIDE] for r in range(CAP)], axis=1)


def by_row(values):
    flat = jnp.concatenate([values[:, r * DOM : (r + 1) * DOM] for r in range(CAP)], axis=0)
    return flat.T


def product(left, head, tail, dims):
    a, b = pieces(left, 2)
    rows = left.shape[0]
    both = mxu(jnp.concatenate([a, b], axis=0), head, dims)
    return both[:rows] + both[rows:] + mxu(a, tail, dims)


def mapped_back(forces, khead, ktail, shell):
    loading = product(forces, khead, ktail, NN) * (1.0 / math.sqrt(PTS))
    shead, stail = pieces(shell, 2)
    displaced = loading + product(loading, shead, stail, NN)
    return product(displaced, khead, ktail, NT) * (1.0 / math.sqrt(NS))


def first_structure_kernel(received, nodes, shell, returned, mapped, khead, ktail):
    for r in range(CAP):
        distance = None
        for c in range(3):
            lane = r * WIDE + 3 + c
            gap = received[:, lane : lane + 1] - nodes[c : c + 1, :]
            distance = gap * gap if distance is None else distance + gap * gap
        weight = jnp.exp(-distance * inv_radius_sq)
        head, tail = pieces(weight, 2)
        khead[r * DOM : (r + 1) * DOM, :] = head
        ktail[r * DOM : (r + 1) * DOM, :] = tail
    held = by_slot(received[...])
    back = mapped_back(held[0:WIDE], khead[...], ktail[...], shell[...])
    mapped[...] = back
    moved = (source_gain * relaxation) * jnp.sum(held[9:12] * (back[0:3] - held[6:9]), axis=0, keepdims=True)
    rows = jnp.concatenate([moved, jnp.zeros((WIDE - 1, NS), f32)], axis=0)
    own = by_row(rows)
    at = lax.broadcasted_iota(i32, own.shape, 0)
    above = jnp.where(at == DOM - 1, 0.0, pltpu.roll(own, DOM - 1, 0))
    below = jnp.where(at == 0, 0.0, pltpu.roll(own, 1, 0))
    both_lanes = own + pltpu.roll(above, 1, 1) + pltpu.roll(below, 2, 1)
    returned[0:DOM] = both_lanes
    returned[DOM : 2 * DOM] = both_lanes


def second_structure_kernel(received, before, mapped, khead, ktail, shell, returned):
    forces = by_slot(received[...])
    held = by_slot(before[...])
    back = mapped_back(forces, khead[...], ktail[...], shell[...])
    t0, t1, d0, used = mapped[0:3, :], back[0:3], held[6:9], held[12:13]
    r0 = t0 - d0
    r1 = t1 - (d0 + relaxation * r0)
    delta = r1 - r0
    sums = []
    for term in (delta * r1, delta * delta, r1 * r1):
        inner = jnp.sum(term * used, axis=0, keepdims=True)
        sums.append(jnp.broadcast_to(jnp.sum(inner, axis=1, keepdims=True), (1, NS)))
    rows = jnp.concatenate([t1, t0, *sums, jnp.zeros((WIDE - 9, NS), f32)], axis=0)
    returned[...] = by_row(rows)


def hand_out_kernel(arrived, meta, out):
    lane = lax.axis_index("lane")
    rows = []
    for tile in range(2):
        owner = lane if tile == 0 else 1 - lane
        held = arrived[pl.ds(pl.multiple_of(owner * DOM, DOM), DOM), :]
        for dx in range(3):
            at = 24 * tile + 18 + 2 * dx
            rows += halves(from_slots(held, joined(meta[at : at + 2]).astype(i32))[dx : dx + 1])
    out[...] = jnp.concatenate([*rows, jnp.zeros((4, 128), f32)], axis=0)


def arrive_kernel(arrived, slot, found, out):
    held = arrived[...]
    found[...] = from_slots(held, slot[...].astype(i32))
    total = jnp.sum(held, axis=0, keepdims=True)
    for k in range(SUB * LANE):
        out[k : k + 1, :] = total


def finish_kernel(found, sums, disp, rms):
    total = jnp.sum(sums[...], axis=0, keepdims=True)
    vr, vv, rr = total[:, 6:7], total[:, 7:8], total[:, 8:9]
    t1, t0 = found[0:3, :], found[3:6, :]
    disp[...] = t1 - (vr / (vv + epsilon)) * (t1 - t0)
    count = 3.0 * PTS * DOM * SUB * LANE
    rms[...] = jnp.sqrt(rr / count)


def shape(*dims, dtype=f32):
    return jax.ShapeDtypeStruct(dims, dtype)


def call(kernel, outs, args, scratch=(), name=None, far=(), far_out=()):
    def spec(k):
        space = pltpu.HBM if k in far else pltpu.VMEM
        return pl.BlockSpec(memory_space=space)

    return pl.pallas_call(
        kernel,
        out_shape=outs,
        in_specs=[spec(k) for k in range(len(args))],
        out_specs=tuple(
            pl.BlockSpec(memory_space=pltpu.HBM if k in far_out else pltpu.VMEM) for k in range(len(outs))
        ),
        scratch_shapes=list(scratch),
        compiler_params=pltpu.CompilerParams(vmem_limit_bytes=40 * 1024 * 1024),
        name=name,
    )(*args)


def body(rhs, coef, pold, cell_index, nrm, coords, partner, nodes, shell, disp):
    cell = cell_index.reshape(1, PTS)
    part = partner.reshape(1, PTS)
    block, main, halo = shape(CX, CY, CZ), shape(CX, RY, CZ), shape(8, RY, CZ)
    row = shape(DOM, CAP * WIDE)
    def swap(across, beside, axis):
        count = lax.axis_size(axis)
        swaps = [(i + k, i + 1 - k) for i in range(1, count - 1, 2) for k in (0, 1)]
        pairs = [[i, i + 1] for i in range(0, count, 2)]
        return lax.ppermute(across, axis, swaps), lax.all_gather(beside, axis, axis_index_groups=pairs)

    def across(rows):
        return lax.all_to_all(rows, "dom", 0, 0, tiled=True)

    face, slab = shape(FACE + 24, CZ), shape(SLAB + RY + 16, CZ)
    src, rden, pold, strips, slot, cell, nrm, disp, coords = call(
        start_kernel,
        (block, block, block, shape(72, CZ), shape(1, PTS), shape(1, PTS, dtype=i32), *[shape(3, PTS)] * 3),
        [pltpu.with_memory_space_constraint(x, pltpu.HBM) for x in (rhs, coef, pold, cell, part, nrm, disp, coords)],
        [pltpu.VMEM((CX, CY, CZ), f32)] * 2 + [pltpu.VMEM((1, PTS), i32), pltpu.SemaphoreType.DMA((8,))],
        name="start",
        far=range(8),
    )
    lanes = lax.all_gather(strips, "lane")
    further, beside = call(faces_kernel, (face, face), (src, rden, pold, cell, lanes), name="sub_faces")
    fromacross, cores = swap(further, beside, "sub")
    beside, further, subhigh, sublow, beyond, tails = call(
        dom_kernel,
        (slab, slab, face, face, shape(4, RY, CZ), shape(16, CZ)),
        (src, rden, pold, cell, slot, fromacross, cores, lanes),
        [pltpu.VMEM((2, SLAB + RY + 16, CZ), f32)],
        name="dom_slabs",
    )
    fromacross, doms = swap(further, beside, "dom")
    esrc, erden, epold, xsrc, xrden, xpold = call(
        ring_kernel, (main,) * 6, (src, rden, pold, subhigh, sublow, beyond), name="ring_fields"
    )
    grid = pltpu.VMEM((RX, RY, CZ), f32)
    pressure, hrden0, hrden1, meta, sending = call(
        first_fluid_kernel,
        (block, halo, halo, shape(48, CZ), row),
        (esrc, erden, epold, xsrc, xrden, xpold, doms, fromacross, tails, cell, nrm, coords, disp, slot),
        [pltpu.VMEM((8, RY, CZ), f32)] * 2 + [pltpu.VMEM((SLAB + RY + 16, CZ), f32)] * 2 + [grid] * 4,
        name="first_fluid",
    )
    received = across(sending)
    square = shape(NS, NS, dtype=bf16)
    returned, mapped, khead, ktail = call(
        first_structure_kernel,
        (shape(2 * DOM, CAP * WIDE), shape(WIDE, NS), square, square),
        (received, nodes, shell),
        name="first_structure",
    )
    arrived = lax.all_to_all(returned, ("lane", "dom"), 0, 0, tiled=True)
    (values,) = call(hand_out_kernel, (shape(16, 128),), (arrived, meta), name="hand_out")
    fromacross, cores = swap(values, values, "sub")
    own_rows = shape(RX, CY, CZ)
    own0, own1 = call(own_rows_kernel, (own_rows, own_rows), (values, meta), name="own_rows")
    pressure, sending = call(
        second_fluid_kernel,
        (block, row),
        (erden, xrden, hrden0, hrden1, pressure, own0, own1, fromacross, cores, meta, cell, nrm, slot),
        [grid] * 6
        + [pltpu.VMEM((CX, CY, CZ), f32), *[pltpu.VMEM((16, 128), f32)] * 2, pltpu.SemaphoreType.DMA],
        name="second_fluid",
        far_out=(0,),
    )
    again = across(sending)
    (returned,) = call(
        second_structure_kernel, (row,), (again, received, mapped, khead, ktail, shell), name="second_structure"
    )
    arrived = across(returned)
    found, sums = call(
        arrive_kernel, (shape(WIDE, PTS), shape(SUB * LANE, 128)), (arrived, slot), name="arrive"
    )
    sums = lax.all_to_all(sums, ("sub", "lane"), 0, 0, tiled=True)
    disp_new, rms = call(finish_kernel, (shape(3, PTS), shape(1, 1)), (found, sums), name="finish")
    return pressure, disp_new, rms.reshape(())


def solution(mesh):
    every = ("dom", "sub", "lane")
    grid, points = P(*every), P(None, every)
    return jax.shard_map(
        body,
        mesh=mesh,
        in_specs=(grid, grid, grid, P(every), points, points, P(every, None), points, P(every, None), points),
        out_specs=(grid, points, P()),
        check_vma=False,
    )
```

```python
import math

import jax
import jax.numpy as jnp
from jax import lax
from jax.experimental import pallas as pl
from jax.experimental.pallas import tpu as pltpu
from jax.sharding import PartitionSpec as P

SWEEPS = 4
DOM, SUB, LANE = 64, 8, 2
CX, CY, CZ = 32, 16, 128
PTS, NS, CAP = 256, 512, 8
RX, RY = CX + 8, CY + 8
WIDE = 16
FACE, SLAB = 10 * CX, 10 * RY

source_gain = 16.0
relaxation = 0.5
inv_radius_sq = 11.111111
epsilon = 1e-06

f32, bf16, i32 = jnp.float32, jnp.bfloat16, jnp.int32
NN = (((1,), (0,)), ((), ()))
NT = (((1,), (1,)), ((), ()))


def pieces(x, count):
    parts = []
    for _ in range(count - 1):
        head = x.astype(bf16)
        parts.append(head)
        x = x - head.astype(f32)
    parts.append(x.astype(bf16))
    return parts


def mxu(a, b, dims):
    return lax.dot_general(a, b, dims, preferred_element_type=f32)


def ones_at(rows, index):
    at = lax.broadcasted_iota(i32, (rows, index.shape[1]), 0)
    return at == index


def as_ones(mask):
    return jnp.where(mask, 1.0, 0.0).astype(bf16)


def spread(rows, z, values, edge=None):
    if edge is None:
        parts = pieces(jnp.where(ones_at(CZ, z), values, 0.0), 2)
    else:
        beside = jnp.where(edge == 0, z, z - (CZ - 16))
        parts = []
        for part in pieces(jnp.where(ones_at(16, beside), values, 0.0), 2):
            zero = jnp.zeros_like(part)
            first, last = jnp.where(edge == 0, part, zero), jnp.where(edge == 0, zero, part)
            parts.append(jnp.concatenate([first, jnp.zeros((CZ - 32, PTS), bf16), last], axis=0))
    total = None
    for part in parts:
        term = mxu(rows, part, NT)
        total = term if total is None else total + term
    return total


def halves(row):
    return row[:, 0:128], row[:, 128:256]


def joined(ref_rows):
    return jnp.concatenate([ref_rows[0:1], ref_rows[1:2]], axis=1)


def up_down(core, beside, across):
    return jnp.where(core == 0, beside, across), jnp.where(core == 0, across, beside)


def start_kernel(
    rhs_far, coef_far, pold_far, cell_far, part_far, nrm_far, disp_far, coords_far,
    src, rden, pold, strips, slot, cell, nrm, disp, coords, rhs, coef, part, sems,
):
    pairs = (
        (cell_far, cell), (part_far, part), (nrm_far, nrm), (disp_far, disp),
        (rhs_far, rhs), (coef_far, coef), (pold_far, pold), (coords_far, coords),
    )
    copies = [pltpu.make_async_copy(a, b, sems.at[k]) for k, (a, b) in enumerate(pairs)]
    for copy in copies:
        copy.start()
    for copy in copies[:4]:
        copy.wait()
    points = cell[...]
    values = source_gain * jnp.sum(disp[...] * nrm[...], axis=0, keepdims=True)
    added = spread(as_ones(ones_at(CX * CY, points >> 7)), points & 127, values)
    owner = ones_at(DOM, part[...])
    earlier = lax.broadcasted_iota(i32, (PTS, PTS), 0) < lax.broadcasted_iota(i32, (PTS, PTS), 1)
    before = mxu(as_ones(owner), as_ones(earlier), NN)
    rank = jnp.sum(jnp.where(owner, before, 0.0), axis=0, keepdims=True)
    slot[...] = part[...].astype(f32) * CAP + rank
    copies[4].wait()
    src[...] = rhs[...] + added.reshape(CX, CY, CZ)
    copies[5].wait()
    rden[...] = 1.0 / (6.0 + coef[...])
    for copy in copies[6:]:
        copy.wait()
    shift = jnp.where(lax.axis_index("lane") == 0, 4, 0)
    at = lax.broadcasted_iota(i32, (CY, CZ), 1)
    for x4 in range(4):
        strips[x4 * CY : (x4 + 1) * CY, :] = packed([lambda k, f=f: f[4 * k + x4] for f in (src, rden, pold)], at, shift)
    tail = [*halves(points.astype(f32)), *halves(slot[...]), jnp.zeros((4, CZ), f32)]
    strips[64:72, :] = jnp.concatenate(tail, axis=0)


def packed(fields, at, shift):
    total = jnp.zeros(at.shape, f32)
    for k in range(8):
        for number, field in enumerate(fields):
            lo = 16 * k + 4 * number
            total = jnp.where((at >= lo) & (at < lo + 4), pltpu.roll(field(k), lax.rem(lo + shift, 128), 1), total)
    return total


def unpacked(rows, lo, lane, keep):
    return jnp.where(keep, pltpu.roll(rows, lax.rem(256 - lo - 4 * lane, 128), 1), 0.0)


def edges(lane, rows):
    at = lax.broadcasted_iota(i32, (rows, CZ), 1)
    return jnp.where(lane == 0, at, CZ - 1 - at) < 4


def faces_kernel(src, rden, pold, cell, lanes, across, beside):
    core, lane = lax.rem(lax.axis_index("sub"), 2), lax.axis_index("lane")
    for field, own, width in ((0, src, 3), (3, rden, 3), (6, pold, 4)):
        for k in range(width):
            at = (field + k) * CX
            low, high = own[:, k, :], own[:, CY - width + k, :]
            beside[at : at + CX, :], across[at : at + CX, :] = up_down(core, high, low)
    other = lanes[1 - lane]
    for x4 in range(4):
        at, low, high = FACE + 4 * x4, other[x4 * CY : x4 * CY + 4], other[(x4 + 1) * CY - 4 : (x4 + 1) * CY]
        beside[at : at + 4, :], across[at : at + 4, :] = up_down(core, high, low)
    tail = jnp.concatenate([*halves(cell[...].astype(f32)), other[64:66], jnp.zeros((4, CZ), f32)], axis=0)
    beside[FACE + 16 : FACE + 24, :] = tail
    across[FACE + 16 : FACE + 24, :] = tail


def dom_kernel(
    src, rden, pold, cell, slot, fromacross, cores, lanes, beside, across, subhigh, sublow, beyond, tails, slabs
):
    core, lane = lax.rem(lax.axis_index("sub"), 2), lax.axis_index("lane")
    subhigh[...], sublow[...] = up_down(core, cores[1 - core], fromacross[...])
    other = lanes[1 - lane]
    cellhigh, celllow = subhigh[FACE + 16 : FACE + 24], sublow[FACE + 16 : FACE + 24]
    tail = [*halves(cell[...].astype(f32)), cellhigh[0:2], celllow[0:2], *halves(slot[...])]
    tails[0:8] = jnp.concatenate(tail, axis=0)
    tails[8:16] = jnp.concatenate([other[64:66], cellhigh[2:4], celllow[2:4], other[66:68]], axis=0)
    for x4 in range(4):
        at = FACE + 4 * x4
        sides = subhigh[at : at + 4], sublow[at : at + 4]
        beyond[x4] = jnp.concatenate([other[x4 * CY : (x4 + 1) * CY], *sides], axis=0)
    at = lax.broadcasted_iota(i32, (RY, CZ), 1)
    low, high = slabs.at[0], slabs.at[1]
    for out, base3, base4, group in ((low, 0, 0, 0), (high, CX - 3, CX - 4, 7)):
        for field, own, width, base in ((0, src, 3, base3), (3, rden, 3, base3), (6, pold, 4, base4)):
            for k in range(width):
                x, row = base + k, (field + k) * RY
                out[row : row + CY, :] = own[x]
                rows = [subhigh[(field + j) * CX + x : (field + j) * CX + x + 1] for j in range(width)]
                rows += [jnp.zeros((1, CZ), f32)] * (8 - 2 * width)
                rows += [sublow[(field + j) * CX + x : (field + j) * CX + x + 1] for j in range(width)]
                out[row + CY : row + RY, :] = jnp.concatenate(rows, axis=0)
        total = jnp.zeros((RY, CZ), f32)
        for j in range(4):
            moved = pltpu.roll(beyond[j], (16 * j - 16 * group) % 128, 1)
            total = jnp.where((at >= 16 * j) & (at < 16 * j + 16), moved, total)
        out[SLAB : SLAB + RY, :] = total
        out[SLAB + RY : SLAB + RY + 16, :] = tails[...]
    beside[...], across[...] = up_down(lax.rem(lax.axis_index("dom"), 2), high[...], low[...])


def near(width):
    return [*range(CX + width), *range(RX - width, RX)]


def ring(own, other, own_halo=None, other_halo=None):
    def layer(x):
        if x < CX or own_halo is None:
            return jnp.concatenate([own[x], other[x]], axis=1)
        return jnp.concatenate([own_halo(x - CX), other_halo[x - CX]], axis=1)

    return layer


def sweep(now, out, source, scale, layers):
    for x in layers:
        here = now(x)
        total = now((x + 1) % RX) + now((x - 1) % RX)
        total = total + (pltpu.roll(here, RY - 1, 0) + pltpu.roll(here, 1, 0))
        total = total + (pltpu.roll(here, 2 * CZ - 1, 1) + pltpu.roll(here, 1, 1))
        total = (source(x) + total) * scale(x)
        out[0][x], out[1][x] = total[:, 0:CZ], total[:, CZ : 2 * CZ]


def last_sweep(now, source, scale, write, layers=range(CX)):
    for x in layers:
        here = now[0][x]
        total = now[0][(x + 1) % RX, 0:CY] + now[0][(x - 1) % RX, 0:CY]
        total = total + (pltpu.roll(here, RY - 1, 0) + pltpu.roll(here, 1, 0))[0:CY]
        wide = jnp.concatenate([here[0:CY], now[1][x, 0:CY]], axis=1)
        beside = pltpu.roll(wide, 2 * CZ - 1, 1) + pltpu.roll(wide, 1, 1)
        write(x, (source[x, 0:CY] + (total + beside[:, 0:CZ])) * scale[x, 0:CY])


def inner(number):
    return range(number, CX - number)


def passed(number):
    return number, number + 1, CX - number - 2, CX - number - 1


def ring_kernel(
    src, rden, pold, subhigh, sublow, beyond,
    esrc, erden, epold, xsrc, xrden, xpold, pressure, kept, even0, even1, odd0, odd1,
):
    for field, own, width, ext in ((0, src, 3, esrc), (3, rden, 3, erden), (6, pold, 4, epold)):
        ext[:, 0:CY, :] = own[...]
        if width == 3:
            ext[:, CY:RY, :] = jnp.zeros((CX, 8, CZ), f32)
        for k in range(width):
            at = (field + k) * CX
            ext[:, CY + k, :] = subhigh[at : at + CX]
            ext[:, RY - width + k, :] = sublow[at : at + CX]
    lane = lax.axis_index("lane")
    keep = edges(lane, RY)
    for x4 in range(4):
        rows = beyond[x4]
        for field, beside in enumerate((xsrc, xrden, xpold)):
            for k in range(8):
                beside[4 * k + x4] = unpacked(rows, 16 * k + 4 * field, lane, keep)
    source, scale = ring(esrc, xsrc), ring(erden, xrden)
    now, spare = (epold, xpold), ((even0, even1), (odd0, odd1))
    for number in (1, 2, 3):
        out = spare[(number - 1) % 2]
        sweep(ring(*now), out, source, scale, inner(number))
        for k, x in enumerate(passed(number)):
            for tile in range(2):
                kept[number - 1, tile, k] = out[tile][x]
        now = out

    def write(x, value):
        pressure[x] = value

    last_sweep(now, esrc, erden, write, inner(4))


def forces_at(pressure, points, nrm):
    at_z = as_ones(ones_at(CZ, points & 127))
    total = None
    for part in pieces(pressure, 2):
        term = mxu(part, at_z, NN)
        total = term if total is None else total + term
    press = jnp.sum(jnp.where(ones_at(CX * CY, points >> 7), total, 0.0), axis=0, keepdims=True)
    return [press * nrm[c : c + 1, :] for c in range(3)]


def first_fluid_kernel(
    esrc, erden, epold, xsrc, xrden, xpold, partly, kept, doms, fromacross, tails, cell, nrm, coords, disp, slot,
    pressure, hrden0, hrden1, meta, sending, hsrc1, hpold1, domhigh, domlow, even0, even1, odd0, odd1,
):
    lane, pair = lax.axis_index("lane"), lax.rem(lax.axis_index("dom"), 2)
    domhigh[...], domlow[...] = up_down(pair, doms[1 - pair], fromacross[...])
    keep = edges(lane, RY)
    for base, slab in ((0, domhigh), (4, domlow)):
        rows = slab[SLAB : SLAB + RY]
        for j in range(4):
            for field, halo in enumerate((hsrc1, hrden1, hpold1)):
                halo[base + j] = unpacked(rows, 16 * j + 4 * field, lane, keep)

    def halo(field, width):
        def layer(x):
            slab, k = (domhigh, x) if x < 4 else (domlow, x - (8 - width))
            return slab[(field + k) * RY : (field + k + 1) * RY]

        return layer

    for x in range(8):
        hrden0[x] = jnp.zeros((RY, CZ), f32) if x in (3, 4) else halo(3, 3)(x)
    source = ring(esrc, xsrc, halo(0, 3), hsrc1)
    scale = ring(erden, xrden, halo(3, 3), hrden1)
    even, odd = (even0, even1), (odd0, odd1)
    now = ring(epold, xpold, halo(6, 4), hpold1)
    for number, out in ((1, even), (2, odd), (3, even)):
        sweep(now, out, source, scale, [x for x in near(4 - number) if x not in inner(number)])
        for k, x in enumerate(passed(number)):
            for tile in range(2):
                out[tile][x] = kept[number - 1, tile, k]
        now = ring(*out)

    def write(x, value):
        pressure[x] = value

    last_sweep(even, esrc, erden, write, [x for x in range(CX) if x not in inner(4)])
    pressure[4 : CX - 4] = partly[4 : CX - 4]
    slots = slot[...].astype(i32)
    values = forces_at(pressure[...].reshape(CX * CY, CZ), cell[...], nrm)
    values += [coords[c : c + 1, :] for c in range(3)]
    values += [disp[c : c + 1, :] for c in range(3)]
    values += [nrm[c : c + 1, :] for c in range(3)]
    values += [jnp.ones((1, PTS), f32)]
    sending[...] = to_slots(values, slots, 3)
    for tile in range(2):
        own = tails[8 * tile : 8 * tile + 8]
        at = SLAB + RY + 8 * tile
        up, down = domhigh[at : at + 8], domlow[at : at + 8]
        meta[24 * tile : 24 * tile + 24] = jnp.concatenate([own[0:6], up[0:6], down[0:6], own[6:], up[6:], down[6:]], axis=0)


def placed(values, points, dx, dy, edge):
    x, y, z = points >> 11, (points >> 7) & 15, points & 127
    if dx == 1:
        x = jnp.where(x < 3, x, -1000)
    elif dx == 2:
        x = jnp.where(x >= CX - 3, x - (CX - 8), -1000)
    if dy == 1:
        y = jnp.where(y < 3, y, -1000000)
    elif dy == 2:
        y = jnp.where(y >= CY - 3, y - (CY - 8), -1000000)
    wide, deep = CY if dy == 0 else 8, CX if dx == 0 else 8
    return spread(as_ones(ones_at(deep * wide, x * wide + y)), z, values, edge).reshape(deep, wide, CZ)


def own_rows_kernel(values, meta, src0, src1):
    lane = lax.axis_index("lane")
    for tile, source in enumerate((src0, src1)):
        parts = []
        for dx in range(3):
            at, row = 6 * tile + 2 * dx, 24 * tile + 6 * dx
            points = joined(meta[row : row + 2]).astype(i32)
            parts.append(placed(joined(values[at : at + 2]), points, dx, 0, None if tile == 0 else lane))
        source[0:CX] = parts[0]
        source[CX:RX] = parts[1] + parts[2]


def second_fluid_kernel(
    erden, xrden, hrden0, hrden1, before, own0, own1, fromacross, cores, meta, cell, nrm, slot,
    pressure_far, sending, src0, src1, even0, even1, odd0, odd1, pressure, fromhigh, fromlow, sems,
):
    lane, core = lax.axis_index("lane"), lax.rem(lax.axis_index("sub"), 2)
    fromhigh[...], fromlow[...] = up_down(core, cores[1 - core], fromacross[...])
    for tile, (source, now, own, scale, halo) in enumerate(
        ((src0, even0, own0, erden, hrden0), (src1, even1, own1, xrden, hrden1))
    ):
        beside = [None] * 3
        for dy, values in ((1, fromhigh), (2, fromlow)):
            for dx in range(3):
                at, row = 6 * tile + 2 * dx, 24 * tile + 6 * dx + 2 * dy
                points = joined(meta[row : row + 2]).astype(i32)
                part = placed(joined(values[at : at + 2]), points, dx, dy, None if tile == 0 else lane)
                beside[dx] = part if dy == 1 else beside[dx] + part
        for ys, part in ((slice(0, CY), own[0:CX]), (slice(CY, RY), beside[0])):
            source[0:CX, ys, :] = part
            now[0:CX, ys, :] = part * scale[:, ys, :]
        for ys, part in ((slice(0, CY), own[CX:RX]), (slice(CY, RY), beside[1] + beside[2])):
            source[CX:RX, ys, :] = part
            now[CX:RX, ys, :] = part * halo[:, ys, :]
    even, odd = (even0, even1), (odd0, odd1)
    source = ring(src0, src1)
    scale = ring(erden, xrden, lambda x: hrden0[x], hrden1)
    sweep(ring(*even), odd, source, scale, near(2))
    sweep(ring(*odd), even, source, scale, near(1))

    def write(x, value):
        pressure[x] = before[x] + value

    copies = []
    for k, x in enumerate(range(0, CX, 8)):
        last_sweep(even, src0, erden, write, range(x, x + 8))
        part = pl.ds(x, 8)
        copies.append(pltpu.make_async_copy(pressure.at[part], pressure_far.at[part], sems.at[k]))
        copies[-1].start()
    sending[...] = to_slots(forces_at(pressure[...].reshape(CX * CY, CZ), cell[...], nrm), slot[...].astype(i32), 2)
    for copy in copies:
        copy.wait()


def to_slots(values, slots, count):
    rank = slots & 7
    filler = [jnp.zeros((1, PTS), f32)] * (WIDE - len(values))
    block = jnp.concatenate(list(values) + filler, axis=0)
    stacked = jnp.concatenate([jnp.where(rank == r, block, 0.0) for r in range(CAP)], axis=0)
    owner = as_ones(ones_at(DOM, slots >> 3))
    total = None
    for part in pieces(stacked, count):
        term = mxu(owner, part, NT)
        total = term if total is None else total + term
    return total


def from_slots(arrived, slots):
    rank = slots & 7
    owner = as_ones(ones_at(DOM, slots >> 3))
    flat = arrived.T
    total = None
    for part in pieces(flat, 2):
        term = mxu(part, owner, NN)
        total = term if total is None else total + term
    found = jnp.zeros((WIDE, PTS), f32)
    for r in range(CAP):
        found = found + jnp.where(rank == r, total[r * WIDE : (r + 1) * WIDE], 0.0)
    return found


def by_slot(received):
    flat = received.T
    return jnp.concatenate([flat[r * WIDE : (r + 1) * WIDE] for r in range(CAP)], axis=1)


def by_row(values):
    flat = jnp.concatenate([values[:, r * DOM : (r + 1) * DOM] for r in range(CAP)], axis=0)
    return flat.T


def product(left, head, tail, dims):
    a, b = pieces(left, 2)
    rows = left.shape[0]
    both = mxu(jnp.concatenate([a, b], axis=0), head, dims)
    return both[:rows] + both[rows:] + mxu(a, tail, dims)


def mapped_back(forces, khead, ktail, shell):
    loading = product(forces, khead, ktail, NN) * (1.0 / math.sqrt(PTS))
    shead, stail = pieces(shell, 2)
    displaced = loading + product(loading, shead, stail, NN)
    return product(displaced, khead, ktail, NT) * (1.0 / math.sqrt(NS))


def first_structure_kernel(received, nodes, shell, returned, mapped, khead, ktail):
    for r in range(CAP):
        distance = None
        for c in range(3):
            lane = r * WIDE + 3 + c
            gap = received[:, lane : lane + 1] - nodes[c : c + 1, :]
            distance = gap * gap if distance is None else distance + gap * gap
        weight = jnp.exp(-distance * inv_radius_sq)
        head, tail = pieces(weight, 2)
        khead[r * DOM : (r + 1) * DOM, :] = head
        ktail[r * DOM : (r + 1) * DOM, :] = tail
    held = by_slot(received[...])
    back = mapped_back(held[0:WIDE], khead[...], ktail[...], shell[...])
    mapped[...] = back
    moved = (source_gain * relaxation) * jnp.sum(held[9:12] * (back[0:3] - held[6:9]), axis=0, keepdims=True)
    rows = jnp.concatenate([moved, jnp.zeros((WIDE - 1, NS), f32)], axis=0)
    own = by_row(rows)
    at = lax.broadcasted_iota(i32, own.shape, 0)
    above = jnp.where(at == DOM - 1, 0.0, pltpu.roll(own, DOM - 1, 0))
    below = jnp.where(at == 0, 0.0, pltpu.roll(own, 1, 0))
    both_lanes = own + pltpu.roll(above, 1, 1) + pltpu.roll(below, 2, 1)
    returned[0:DOM] = both_lanes
    returned[DOM : 2 * DOM] = both_lanes


def second_structure_kernel(received, before, mapped, khead, ktail, shell, returned):
    forces = by_slot(received[...])
    held = by_slot(before[...])
    back = mapped_back(forces, khead[...], ktail[...], shell[...])
    t0, t1, d0, used = mapped[0:3, :], back[0:3], held[6:9], held[12:13]
    r0 = t0 - d0
    r1 = t1 - (d0 + relaxation * r0)
    delta = r1 - r0
    sums = []
    for term in (delta * r1, delta * delta, r1 * r1):
        inner = jnp.sum(term * used, axis=0, keepdims=True)
        sums.append(jnp.broadcast_to(jnp.sum(inner, axis=1, keepdims=True), (1, NS)))
    rows = jnp.concatenate([t1, t0, *sums, jnp.zeros((WIDE - 9, NS), f32)], axis=0)
    returned[...] = by_row(rows)


def hand_out_kernel(arrived, meta, out):
    lane = lax.axis_index("lane")
    rows = []
    for tile in range(2):
        owner = lane if tile == 0 else 1 - lane
        held = arrived[pl.ds(pl.multiple_of(owner * DOM, DOM), DOM), :]
        for dx in range(3):
            at = 24 * tile + 18 + 2 * dx
            rows += halves(from_slots(held, joined(meta[at : at + 2]).astype(i32))[dx : dx + 1])
    out[...] = jnp.concatenate([*rows, jnp.zeros((4, 128), f32)], axis=0)


def arrive_kernel(arrived, slot, found, out):
    held = arrived[...]
    found[...] = from_slots(held, slot[...].astype(i32))
    total = jnp.sum(held, axis=0, keepdims=True)
    for k in range(SUB * LANE):
        out[k : k + 1, :] = total


def finish_kernel(found, sums, disp, rms):
    total = jnp.sum(sums[...], axis=0, keepdims=True)
    vr, vv, rr = total[:, 6:7], total[:, 7:8], total[:, 8:9]
    t1, t0 = found[0:3, :], found[3:6, :]
    disp[...] = t1 - (vr / (vv + epsilon)) * (t1 - t0)
    count = 3.0 * PTS * DOM * SUB * LANE
    rms[...] = jnp.sqrt(rr / count)


def shape(*dims, dtype=f32):
    return jax.ShapeDtypeStruct(dims, dtype)


def call(kernel, outs, args, scratch=(), name=None, far=(), far_out=()):
    def spec(k):
        space = pltpu.HBM if k in far else pltpu.VMEM
        return pl.BlockSpec(memory_space=space)

    return pl.pallas_call(
        kernel,
        out_shape=outs,
        in_specs=[spec(k) for k in range(len(args))],
        out_specs=tuple(
            pl.BlockSpec(memory_space=pltpu.HBM if k in far_out else pltpu.VMEM) for k in range(len(outs))
        ),
        scratch_shapes=list(scratch),
        compiler_params=pltpu.CompilerParams(vmem_limit_bytes=40 * 1024 * 1024),
        name=name,
    )(*args)


def body(rhs, coef, pold, cell_index, nrm, coords, partner, nodes, shell, disp):
    cell = cell_index.reshape(1, PTS)
    part = partner.reshape(1, PTS)
    block, main, halo = shape(CX, CY, CZ), shape(CX, RY, CZ), shape(8, RY, CZ)
    row = shape(DOM, CAP * WIDE)
    def swap(across, beside, axis):
        count = lax.axis_size(axis)
        swaps = [(i + k, i + 1 - k) for i in range(1, count - 1, 2) for k in (0, 1)]
        pairs = [[i, i + 1] for i in range(0, count, 2)]
        return lax.ppermute(across, axis, swaps), lax.all_gather(beside, axis, axis_index_groups=pairs)

    def across(rows):
        return lax.all_to_all(rows, "dom", 0, 0, tiled=True)

    face, slab = shape(FACE + 24, CZ), shape(SLAB + RY + 16, CZ)
    src, rden, pold, strips, slot, cell, nrm, disp, coords = call(
        start_kernel,
        (block, block, block, shape(72, CZ), shape(1, PTS), shape(1, PTS, dtype=i32), *[shape(3, PTS)] * 3),
        [pltpu.with_memory_space_constraint(x, pltpu.HBM) for x in (rhs, coef, pold, cell, part, nrm, disp, coords)],
        [pltpu.VMEM((CX, CY, CZ), f32)] * 2 + [pltpu.VMEM((1, PTS), i32), pltpu.SemaphoreType.DMA((8,))],
        name="start",
        far=range(8),
    )
    lanes = lax.all_gather(strips, "lane")
    further, beside = call(faces_kernel, (face, face), (src, rden, pold, cell, lanes), name="sub_faces")
    fromacross, cores = swap(further, beside, "sub")
    square = shape(NS, NS, dtype=bf16)
    beside, further, subhigh, sublow, beyond, tails = call(
        dom_kernel,
        (slab, slab, face, face, shape(4, RY, CZ), shape(16, CZ)),
        (src, rden, pold, cell, slot, fromacross, cores, lanes),
        [pltpu.VMEM((2, SLAB + RY + 16, CZ), f32)],
        name="dom_slabs",
    )
    fromacross, doms = swap(further, beside, "dom")
    grid = pltpu.VMEM((RX, RY, CZ), f32)
    esrc, erden, epold, xsrc, xrden, xpold, partly, kept = call(
        ring_kernel,
        (*[main] * 6, block, shape(3, 2, 4, RY, CZ)),
        (src, rden, pold, subhigh, sublow, beyond),
        [pltpu.VMEM((CX, RY, CZ), f32)] * 4,
        name="ring_fields",
    )
    pressure, hrden0, hrden1, meta, sending = call(
        first_fluid_kernel,
        (block, halo, halo, shape(48, CZ), row),
        (esrc, erden, epold, xsrc, xrden, xpold, partly, kept, doms, fromacross, tails, cell, nrm, coords, disp, slot),
        [pltpu.VMEM((8, RY, CZ), f32)] * 2 + [pltpu.VMEM((SLAB + RY + 16, CZ), f32)] * 2 + [grid] * 4,
        name="first_fluid",
    )
    received = across(sending)
    returned, mapped, khead, ktail = call(
        first_structure_kernel,
        (shape(2 * DOM, CAP * WIDE), shape(WIDE, NS), square, square),
        (received, nodes, shell),
        name="first_structure",
    )
    arrived = lax.all_to_all(returned, ("lane", "dom"), 0, 0, tiled=True)
    (values,) = call(hand_out_kernel, (shape(16, 128),), (arrived, meta), name="hand_out")
    fromacross, cores = swap(values, values, "sub")
    own_rows = shape(RX, CY, CZ)
    own0, own1 = call(own_rows_kernel, (own_rows, own_rows), (values, meta), name="own_rows")
    pressure, sending = call(
        second_fluid_kernel,
        (block, row),
        (erden, xrden, hrden0, hrden1, pressure, own0, own1, fromacross, cores, meta, cell, nrm, slot),
        [grid] * 6
        + [pltpu.VMEM((CX, CY, CZ), f32), *[pltpu.VMEM((16, 128), f32)] * 2, pltpu.SemaphoreType.DMA((4,))],
        name="second_fluid",
        far_out=(0,),
    )
    again = across(sending)
    (returned,) = call(
        second_structure_kernel, (row,), (again, received, mapped, khead, ktail, shell), name="second_structure"
    )
    arrived = across(returned)
    found, sums = call(
        arrive_kernel, (shape(WIDE, PTS), shape(SUB * LANE, 128)), (arrived, slot), name="arrive"
    )
    sums = lax.all_to_all(sums, ("sub", "lane"), 0, 0, tiled=True)
    disp_new, rms = call(finish_kernel, (shape(3, PTS), shape(1, 1)), (found, sums), name="finish")
    return pressure, disp_new, rms.reshape(())


def solution(mesh):
    every = ("dom", "sub", "lane")
    grid, points = P(*every), P(None, every)
    return jax.shard_map(
        body,
        mesh=mesh,
        in_specs=(grid, grid, grid, P(every), points, points, P(every, None), points, P(every, None), points),
        out_specs=(grid, points, P()),
        check_vma=False,
    )
```

```python
import math

import jax
import jax.numpy as jnp
from jax import lax
from jax.experimental import pallas as pl
from jax.experimental.pallas import tpu as pltpu
from jax.sharding import PartitionSpec as P

SWEEPS = 4
DOM, SUB, LANE = 64, 8, 2
CX, CY, CZ = 32, 16, 128
PTS, NS, CAP = 256, 512, 8
RX, RY = CX + 8, CY + 8
WIDE = 16
FACE, SLAB = 10 * CX, 10 * RY

source_gain = 16.0
relaxation = 0.5
inv_radius_sq = 11.111111
epsilon = 1e-06

f32, bf16, i32 = jnp.float32, jnp.bfloat16, jnp.int32
NN = (((1,), (0,)), ((), ()))
NT = (((1,), (1,)), ((), ()))


def pieces(x, count):
    parts = []
    for _ in range(count - 1):
        head = x.astype(bf16)
        parts.append(head)
        x = x - head.astype(f32)
    parts.append(x.astype(bf16))
    return parts


def mxu(a, b, dims):
    return lax.dot_general(a, b, dims, preferred_element_type=f32)


def ones_at(rows, index):
    at = lax.broadcasted_iota(i32, (rows, index.shape[1]), 0)
    return at == index


def as_ones(mask):
    return jnp.where(mask, 1.0, 0.0).astype(bf16)


def spread(rows, z, values, edge=None):
    if edge is None:
        parts = pieces(jnp.where(ones_at(CZ, z), values, 0.0), 2)
    else:
        beside = jnp.where(edge == 0, z, z - (CZ - 16))
        parts = []
        for part in pieces(jnp.where(ones_at(16, beside), values, 0.0), 2):
            zero = jnp.zeros_like(part)
            first, last = jnp.where(edge == 0, part, zero), jnp.where(edge == 0, zero, part)
            parts.append(jnp.concatenate([first, jnp.zeros((CZ - 32, PTS), bf16), last], axis=0))
    total = None
    for part in parts:
        term = mxu(rows, part, NT)
        total = term if total is None else total + term
    return total


def halves(row):
    return row[:, 0:128], row[:, 128:256]


def joined(ref_rows):
    return jnp.concatenate([ref_rows[0:1], ref_rows[1:2]], axis=1)


def up_down(core, beside, across):
    return jnp.where(core == 0, beside, across), jnp.where(core == 0, across, beside)


def start_kernel(
    rhs_far, coef_far, pold_far, cell_far, part_far, nrm_far, disp_far, coords_far,
    src, rden, pold, across, strips, slot, cell, nrm, disp, coords, rhs, coef, part, sems,
):
    pairs = (
        (cell_far, cell), (part_far, part), (nrm_far, nrm), (disp_far, disp),
        (rhs_far, rhs), (coef_far, coef), (pold_far, pold), (coords_far, coords),
    )
    copies = [pltpu.make_async_copy(a, b, sems.at[k]) for k, (a, b) in enumerate(pairs)]
    for copy in copies:
        copy.start()
    for copy in copies[:4]:
        copy.wait()
    points = cell[...]
    values = source_gain * jnp.sum(disp[...] * nrm[...], axis=0, keepdims=True)
    added = spread(as_ones(ones_at(CX * CY, points >> 7)), points & 127, values)
    owner = ones_at(DOM, part[...])
    earlier = lax.broadcasted_iota(i32, (PTS, PTS), 0) < lax.broadcasted_iota(i32, (PTS, PTS), 1)
    before = mxu(as_ones(owner), as_ones(earlier), NN)
    rank = jnp.sum(jnp.where(owner, before, 0.0), axis=0, keepdims=True)
    slot[...] = part[...].astype(f32) * CAP + rank
    copies[4].wait()
    src[...] = rhs[...] + added.reshape(CX, CY, CZ)
    copies[5].wait()
    rden[...] = 1.0 / (6.0 + coef[...])
    for copy in copies[6:]:
        copy.wait()
    core = lax.rem(lax.axis_index("sub"), 2)
    for field, own, width in ((0, src, 3), (3, rden, 3), (6, pold, 4)):
        for k in range(width):
            at = (field + k) * CX
            across[at : at + CX, :] = jnp.where(core == 0, own[:, k, :], own[:, CY - width + k, :])
    shift = jnp.where(lax.axis_index("lane") == 0, 4, 0)
    at = lax.broadcasted_iota(i32, (CY, CZ), 1)
    for x4 in range(4):
        strips[x4 * CY : (x4 + 1) * CY, :] = packed([lambda k, f=f: f[4 * k + x4] for f in (src, rden, pold)], at, shift)
    tail = [*halves(points.astype(f32)), *halves(slot[...]), jnp.zeros((4, CZ), f32)]
    strips[64:72, :] = jnp.concatenate(tail, axis=0)


def packed(fields, at, shift):
    total = jnp.zeros(at.shape, f32)
    for k in range(8):
        for number, field in enumerate(fields):
            lo = 16 * k + 4 * number
            total = jnp.where((at >= lo) & (at < lo + 4), pltpu.roll(field(k), lax.rem(lo + shift, 128), 1), total)
    return total


def unpacked(rows, lo, lane, keep):
    return jnp.where(keep, pltpu.roll(rows, lax.rem(256 - lo - 4 * lane, 128), 1), 0.0)


def edges(lane, rows):
    at = lax.broadcasted_iota(i32, (rows, CZ), 1)
    return jnp.where(lane == 0, at, CZ - 1 - at) < 4


def faces_kernel(src, rden, pold, cell, lanes, extra, beside):
    core, lane = lax.rem(lax.axis_index("sub"), 2), lax.axis_index("lane")
    for field, own, width in ((0, src, 3), (3, rden, 3), (6, pold, 4)):
        for k in range(width):
            at = (field + k) * CX
            beside[at : at + CX, :] = jnp.where(core == 0, own[:, CY - width + k, :], own[:, k, :])
    other = lanes[1 - lane]
    for x4 in range(4):
        at, low, high = 4 * x4, other[x4 * CY : x4 * CY + 4], other[(x4 + 1) * CY - 4 : (x4 + 1) * CY]
        beside[FACE + at : FACE + at + 4, :], extra[at : at + 4, :] = up_down(core, high, low)
    tail = jnp.concatenate([*halves(cell[...].astype(f32)), other[64:66], jnp.zeros((4, CZ), f32)], axis=0)
    beside[FACE + 16 : FACE + 24, :] = tail
    extra[16:24, :] = tail


def dom_kernel(
    src, rden, pold, cell, slot, fromacross, extra, cores, lanes, beside, across, subhigh, sublow, beyond, tails, slabs
):
    core, lane = lax.rem(lax.axis_index("sub"), 2), lax.axis_index("lane")
    for rows, far in ((slice(0, FACE), fromacross), (slice(FACE, FACE + 24), extra)):
        subhigh[rows], sublow[rows] = up_down(core, cores[1 - core, rows], far[...])
    other = lanes[1 - lane]
    cellhigh, celllow = subhigh[FACE + 16 : FACE + 24], sublow[FACE + 16 : FACE + 24]
    tail = [*halves(cell[...].astype(f32)), cellhigh[0:2], celllow[0:2], *halves(slot[...])]
    tails[0:8] = jnp.concatenate(tail, axis=0)
    tails[8:16] = jnp.concatenate([other[64:66], cellhigh[2:4], celllow[2:4], other[66:68]], axis=0)
    for x4 in range(4):
        at = FACE + 4 * x4
        sides = subhigh[at : at + 4], sublow[at : at + 4]
        beyond[x4] = jnp.concatenate([other[x4 * CY : (x4 + 1) * CY], *sides], axis=0)
    at = lax.broadcasted_iota(i32, (RY, CZ), 1)
    low, high = slabs.at[0], slabs.at[1]
    for out, base3, base4, group in ((low, 0, 0, 0), (high, CX - 3, CX - 4, 7)):
        for field, own, width, base in ((0, src, 3, base3), (3, rden, 3, base3), (6, pold, 4, base4)):
            for k in range(width):
                x, row = base + k, (field + k) * RY
                out[row : row + CY, :] = own[x]
                rows = [subhigh[(field + j) * CX + x : (field + j) * CX + x + 1] for j in range(width)]
                rows += [jnp.zeros((1, CZ), f32)] * (8 - 2 * width)
                rows += [sublow[(field + j) * CX + x : (field + j) * CX + x + 1] for j in range(width)]
                out[row + CY : row + RY, :] = jnp.concatenate(rows, axis=0)
        total = jnp.zeros((RY, CZ), f32)
        for j in range(4):
            moved = pltpu.roll(beyond[j], (16 * j - 16 * group) % 128, 1)
            total = jnp.where((at >= 16 * j) & (at < 16 * j + 16), moved, total)
        out[SLAB : SLAB + RY, :] = total
        out[SLAB + RY : SLAB + RY + 16, :] = tails[...]
    beside[...], across[...] = up_down(lax.rem(lax.axis_index("dom"), 2), high[...], low[...])


def near(width):
    return [*range(CX + width), *range(RX - width, RX)]


def ring(own, other, own_halo=None, other_halo=None):
    def layer(x):
        if x < CX or own_halo is None:
            return jnp.concatenate([own[x], other[x]], axis=1)
        return jnp.concatenate([own_halo(x - CX), other_halo[x - CX]], axis=1)

    return layer


def sweep(now, out, source, scale, layers):
    for x in layers:
        here = now(x)
        total = now((x + 1) % RX) + now((x - 1) % RX)
        total = total + (pltpu.roll(here, RY - 1, 0) + pltpu.roll(here, 1, 0))
        total = total + (pltpu.roll(here, 2 * CZ - 1, 1) + pltpu.roll(here, 1, 1))
        total = (source(x) + total) * scale(x)
        out[0][x], out[1][x] = total[:, 0:CZ], total[:, CZ : 2 * CZ]


def last_sweep(now, source, scale, write, layers=range(CX)):
    for x in layers:
        here = now[0][x]
        total = now[0][(x + 1) % RX, 0:CY] + now[0][(x - 1) % RX, 0:CY]
        total = total + (pltpu.roll(here, RY - 1, 0) + pltpu.roll(here, 1, 0))[0:CY]
        wide = jnp.concatenate([here[0:CY], now[1][x, 0:CY]], axis=1)
        beside = pltpu.roll(wide, 2 * CZ - 1, 1) + pltpu.roll(wide, 1, 1)
        write(x, (source[x, 0:CY] + (total + beside[:, 0:CZ])) * scale[x, 0:CY])


def inner(number):
    return range(number, CX - number)


def passed(number):
    return number, number + 1, CX - number - 2, CX - number - 1


def ring_kernel(
    src, rden, pold, subhigh, sublow, beyond,
    esrc, erden, epold, xsrc, xrden, xpold, pressure, kept, even0, even1, odd0, odd1,
):
    for field, own, width, ext in ((0, src, 3, esrc), (3, rden, 3, erden), (6, pold, 4, epold)):
        ext[:, 0:CY, :] = own[...]
        if width == 3:
            ext[:, CY:RY, :] = jnp.zeros((CX, 8, CZ), f32)
        for k in range(width):
            at = (field + k) * CX
            ext[:, CY + k, :] = subhigh[at : at + CX]
            ext[:, RY - width + k, :] = sublow[at : at + CX]
    lane = lax.axis_index("lane")
    keep = edges(lane, RY)
    for x4 in range(4):
        rows = beyond[x4]
        for field, beside in enumerate((xsrc, xrden, xpold)):
            for k in range(8):
                beside[4 * k + x4] = unpacked(rows, 16 * k + 4 * field, lane, keep)
    source, scale = ring(esrc, xsrc), ring(erden, xrden)
    now, spare = (epold, xpold), ((even0, even1), (odd0, odd1))
    for number in (1, 2, 3):
        out = spare[(number - 1) % 2]
        sweep(ring(*now), out, source, scale, inner(number))
        for k, x in enumerate(passed(number)):
            for tile in range(2):
                kept[number - 1, tile, k] = out[tile][x]
        now = out

    def write(x, value):
        pressure[x] = value

    last_sweep(now, esrc, erden, write, inner(4))


def forces_at(pressure, points, nrm):
    at_z = as_ones(ones_at(CZ, points & 127))
    total = None
    for part in pieces(pressure, 2):
        term = mxu(part, at_z, NN)
        total = term if total is None else total + term
    press = jnp.sum(jnp.where(ones_at(CX * CY, points >> 7), total, 0.0), axis=0, keepdims=True)
    return [press * nrm[c : c + 1, :] for c in range(3)]


def first_fluid_kernel(
    esrc, erden, epold, xsrc, xrden, xpold, partly, kept, doms, fromacross, tails, cell, nrm, coords, disp, slot,
    pressure, hrden0, hrden1, meta, sending, hsrc1, hpold1, domhigh, domlow, even0, even1, odd0, odd1,
):
    lane, pair = lax.axis_index("lane"), lax.rem(lax.axis_index("dom"), 2)
    domhigh[...], domlow[...] = up_down(pair, doms[1 - pair], fromacross[...])
    keep = edges(lane, RY)
    for base, slab in ((0, domhigh), (4, domlow)):
        rows = slab[SLAB : SLAB + RY]
        for j in range(4):
            for field, halo in enumerate((hsrc1, hrden1, hpold1)):
                halo[base + j] = unpacked(rows, 16 * j + 4 * field, lane, keep)

    def halo(field, width):
        def layer(x):
            slab, k = (domhigh, x) if x < 4 else (domlow, x - (8 - width))
            return slab[(field + k) * RY : (field + k + 1) * RY]

        return layer

    for x in range(8):
        hrden0[x] = jnp.zeros((RY, CZ), f32) if x in (3, 4) else halo(3, 3)(x)
    source = ring(esrc, xsrc, halo(0, 3), hsrc1)
    scale = ring(erden, xrden, halo(3, 3), hrden1)
    even, odd = (even0, even1), (odd0, odd1)
    now = ring(epold, xpold, halo(6, 4), hpold1)
    for number, out in ((1, even), (2, odd), (3, even)):
        sweep(now, out, source, scale, [x for x in near(4 - number) if x not in inner(number)])
        for k, x in enumerate(passed(number)):
            for tile in range(2):
                out[tile][x] = kept[number - 1, tile, k]
        now = ring(*out)

    def write(x, value):
        pressure[x] = value

    last_sweep(even, esrc, erden, write, [x for x in range(CX) if x not in inner(4)])
    pressure[4 : CX - 4] = partly[4 : CX - 4]
    slots = slot[...].astype(i32)
    values = forces_at(pressure[...].reshape(CX * CY, CZ), cell[...], nrm)
    values += [coords[c : c + 1, :] for c in range(3)]
    values += [disp[c : c + 1, :] for c in range(3)]
    values += [nrm[c : c + 1, :] for c in range(3)]
    values += [jnp.ones((1, PTS), f32)]
    sending[...] = to_slots(values, slots, 3)
    for tile in range(2):
        own = tails[8 * tile : 8 * tile + 8]
        at = SLAB + RY + 8 * tile
        up, down = domhigh[at : at + 8], domlow[at : at + 8]
        meta[24 * tile : 24 * tile + 24] = jnp.concatenate([own[0:6], up[0:6], down[0:6], own[6:], up[6:], down[6:]], axis=0)


def placed(values, points, dx, dy, edge):
    x, y, z = points >> 11, (points >> 7) & 15, points & 127
    if dx == 1:
        x = jnp.where(x < 3, x, -1000)
    elif dx == 2:
        x = jnp.where(x >= CX - 3, x - (CX - 8), -1000)
    if dy == 1:
        y = jnp.where(y < 3, y, -1000000)
    elif dy == 2:
        y = jnp.where(y >= CY - 3, y - (CY - 8), -1000000)
    wide, deep = CY if dy == 0 else 8, CX if dx == 0 else 8
    return spread(as_ones(ones_at(deep * wide, x * wide + y)), z, values, edge).reshape(deep, wide, CZ)


def own_rows_kernel(values, meta, src0, src1):
    lane = lax.axis_index("lane")
    for tile, source in enumerate((src0, src1)):
        parts = []
        for dx in range(3):
            at, row = 6 * tile + 2 * dx, 24 * tile + 6 * dx
            points = joined(meta[row : row + 2]).astype(i32)
            parts.append(placed(joined(values[at : at + 2]), points, dx, 0, None if tile == 0 else lane))
        source[0:CX] = parts[0]
        source[CX:RX] = parts[1] + parts[2]


def second_fluid_kernel(
    erden, xrden, hrden0, hrden1, before, own0, own1, fromacross, cores, meta, cell, nrm, slot,
    pressure_far, sending, src0, src1, even0, even1, odd0, odd1, pressure, fromhigh, fromlow, sems,
):
    lane, core = lax.axis_index("lane"), lax.rem(lax.axis_index("sub"), 2)
    fromhigh[...], fromlow[...] = up_down(core, cores[1 - core], fromacross[...])
    for tile, (source, now, own, scale, halo) in enumerate(
        ((src0, even0, own0, erden, hrden0), (src1, even1, own1, xrden, hrden1))
    ):
        beside = [None] * 3
        for dy, values in ((1, fromhigh), (2, fromlow)):
            for dx in range(3):
                at, row = 6 * tile + 2 * dx, 24 * tile + 6 * dx + 2 * dy
                points = joined(meta[row : row + 2]).astype(i32)
                part = placed(joined(values[at : at + 2]), points, dx, dy, None if tile == 0 else lane)
                beside[dx] = part if dy == 1 else beside[dx] + part
        for ys, part in ((slice(0, CY), own[0:CX]), (slice(CY, RY), beside[0])):
            source[0:CX, ys, :] = part
            now[0:CX, ys, :] = part * scale[:, ys, :]
        for ys, part in ((slice(0, CY), own[CX:RX]), (slice(CY, RY), beside[1] + beside[2])):
            source[CX:RX, ys, :] = part
            now[CX:RX, ys, :] = part * halo[:, ys, :]
    even, odd = (even0, even1), (odd0, odd1)
    source = ring(src0, src1)
    scale = ring(erden, xrden, lambda x: hrden0[x], hrden1)
    sweep(ring(*even), odd, source, scale, near(2))
    sweep(ring(*odd), even, source, scale, near(1))

    def write(x, value):
        pressure[x] = before[x] + value

    copies = []
    for k, x in enumerate(range(0, CX, 8)):
        last_sweep(even, src0, erden, write, range(x, x + 8))
        part = pl.ds(x, 8)
        copies.append(pltpu.make_async_copy(pressure.at[part], pressure_far.at[part], sems.at[k]))
        copies[-1].start()
    sending[...] = to_slots(forces_at(pressure[...].reshape(CX * CY, CZ), cell[...], nrm), slot[...].astype(i32), 2)
    for copy in copies:
        copy.wait()


def to_slots(values, slots, count):
    rank = slots & 7
    filler = [jnp.zeros((1, PTS), f32)] * (WIDE - len(values))
    block = jnp.concatenate(list(values) + filler, axis=0)
    stacked = jnp.concatenate([jnp.where(rank == r, block, 0.0) for r in range(CAP)], axis=0)
    owner = as_ones(ones_at(DOM, slots >> 3))
    total = None
    for part in pieces(stacked, count):
        term = mxu(owner, part, NT)
        total = term if total is None else total + term
    return total


def from_slots(arrived, slots):
    rank = slots & 7
    owner = as_ones(ones_at(DOM, slots >> 3))
    flat = arrived.T
    total = None
    for part in pieces(flat, 2):
        term = mxu(part, owner, NN)
        total = term if total is None else total + term
    found = jnp.zeros((WIDE, PTS), f32)
    for r in range(CAP):
        found = found + jnp.where(rank == r, total[r * WIDE : (r + 1) * WIDE], 0.0)
    return found


def by_slot(received):
    flat = received.T
    return jnp.concatenate([flat[r * WIDE : (r + 1) * WIDE] for r in range(CAP)], axis=1)


def by_row(values):
    flat = jnp.concatenate([values[:, r * DOM : (r + 1) * DOM] for r in range(CAP)], axis=0)
    return flat.T


def product(left, head, tail, dims):
    a, b = pieces(left, 2)
    rows = left.shape[0]
    both = mxu(jnp.concatenate([a, b], axis=0), head, dims)
    return both[:rows] + both[rows:] + mxu(a, tail, dims)


def mapped_back(forces, khead, ktail, shell):
    loading = product(forces, khead, ktail, NN) * (1.0 / math.sqrt(PTS))
    shead, stail = pieces(shell, 2)
    displaced = loading + product(loading, shead, stail, NN)
    return product(displaced, khead, ktail, NT) * (1.0 / math.sqrt(NS))


def first_structure_kernel(received, nodes, shell, returned, mapped, khead, ktail):
    for r in range(CAP):
        distance = None
        for c in range(3):
            lane = r * WIDE + 3 + c
            gap = received[:, lane : lane + 1] - nodes[c : c + 1, :]
            distance = gap * gap if distance is None else distance + gap * gap
        weight = jnp.exp(-distance * inv_radius_sq)
        head, tail = pieces(weight, 2)
        khead[r * DOM : (r + 1) * DOM, :] = head
        ktail[r * DOM : (r + 1) * DOM, :] = tail
    held = by_slot(received[...])
    back = mapped_back(held[0:WIDE], khead[...], ktail[...], shell[...])
    mapped[...] = back
    moved = (source_gain * relaxation) * jnp.sum(held[9:12] * (back[0:3] - held[6:9]), axis=0, keepdims=True)
    rows = jnp.concatenate([moved, jnp.zeros((WIDE - 1, NS), f32)], axis=0)
    own = by_row(rows)
    at = lax.broadcasted_iota(i32, own.shape, 0)
    above = jnp.where(at == DOM - 1, 0.0, pltpu.roll(own, DOM - 1, 0))
    below = jnp.where(at == 0, 0.0, pltpu.roll(own, 1, 0))
    both_lanes = own + pltpu.roll(above, 1, 1) + pltpu.roll(below, 2, 1)
    returned[0:DOM] = both_lanes
    returned[DOM : 2 * DOM] = both_lanes


def second_structure_kernel(received, before, mapped, khead, ktail, shell, returned):
    forces = by_slot(received[...])
    held = by_slot(before[...])
    back = mapped_back(forces, khead[...], ktail[...], shell[...])
    t0, t1, d0, used = mapped[0:3, :], back[0:3], held[6:9], held[12:13]
    r0 = t0 - d0
    r1 = t1 - (d0 + relaxation * r0)
    delta = r1 - r0
    sums = []
    for term in (delta * r1, delta * delta, r1 * r1):
        inner = jnp.sum(term * used, axis=0, keepdims=True)
        sums.append(jnp.broadcast_to(jnp.sum(inner, axis=1, keepdims=True), (1, NS)))
    rows = jnp.concatenate([t1, t0, *sums, jnp.zeros((WIDE - 9, NS), f32)], axis=0)
    returned[...] = by_row(rows)


def hand_out_kernel(arrived, meta, out):
    lane = lax.axis_index("lane")
    rows = []
    for tile in range(2):
        owner = lane if tile == 0 else 1 - lane
        held = arrived[pl.ds(pl.multiple_of(owner * DOM, DOM), DOM), :]
        for dx in range(3):
            at = 24 * tile + 18 + 2 * dx
            rows += halves(from_slots(held, joined(meta[at : at + 2]).astype(i32))[dx : dx + 1])
    out[...] = jnp.concatenate([*rows, jnp.zeros((4, 128), f32)], axis=0)


def arrive_kernel(arrived, slot, found, out):
    held = arrived[...]
    found[...] = from_slots(held, slot[...].astype(i32))
    total = jnp.sum(held, axis=0, keepdims=True)
    for k in range(SUB * LANE):
        out[k : k + 1, :] = total


def finish_kernel(found, sums, disp, rms):
    total = jnp.sum(sums[...], axis=0, keepdims=True)
    vr, vv, rr = total[:, 6:7], total[:, 7:8], total[:, 8:9]
    t1, t0 = found[0:3, :], found[3:6, :]
    disp[...] = t1 - (vr / (vv + epsilon)) * (t1 - t0)
    count = 3.0 * PTS * DOM * SUB * LANE
    rms[...] = jnp.sqrt(rr / count)


def shape(*dims, dtype=f32):
    return jax.ShapeDtypeStruct(dims, dtype)


def call(kernel, outs, args, scratch=(), name=None, far=(), far_out=()):
    def spec(k):
        space = pltpu.HBM if k in far else pltpu.VMEM
        return pl.BlockSpec(memory_space=space)

    return pl.pallas_call(
        kernel,
        out_shape=outs,
        in_specs=[spec(k) for k in range(len(args))],
        out_specs=tuple(
            pl.BlockSpec(memory_space=pltpu.HBM if k in far_out else pltpu.VMEM) for k in range(len(outs))
        ),
        scratch_shapes=list(scratch),
        compiler_params=pltpu.CompilerParams(vmem_limit_bytes=40 * 1024 * 1024),
        name=name,
    )(*args)


def body(rhs, coef, pold, cell_index, nrm, coords, partner, nodes, shell, disp):
    cell = cell_index.reshape(1, PTS)
    part = partner.reshape(1, PTS)
    block, main, halo = shape(CX, CY, CZ), shape(CX, RY, CZ), shape(8, RY, CZ)
    row = shape(DOM, CAP * WIDE)
    def swap(across, beside, axis):
        count = lax.axis_size(axis)
        swaps = [(i + k, i + 1 - k) for i in range(1, count - 1, 2) for k in (0, 1)]
        pairs = [[i, i + 1] for i in range(0, count, 2)]
        return lax.ppermute(across, axis, swaps), lax.all_gather(beside, axis, axis_index_groups=pairs)

    def across(rows):
        return lax.all_to_all(rows, "dom", 0, 0, tiled=True)

    face, slab = shape(FACE + 24, CZ), shape(SLAB + RY + 16, CZ)
    src, rden, pold, further, strips, slot, cell, nrm, disp, coords = call(
        start_kernel,
        (block, block, block, shape(FACE, CZ), shape(72, CZ), shape(1, PTS), shape(1, PTS, dtype=i32), *[shape(3, PTS)] * 3),
        [pltpu.with_memory_space_constraint(x, pltpu.HBM) for x in (rhs, coef, pold, cell, part, nrm, disp, coords)],
        [pltpu.VMEM((CX, CY, CZ), f32)] * 2 + [pltpu.VMEM((1, PTS), i32), pltpu.SemaphoreType.DMA((8,))],
        name="start",
        far=range(8),
    )
    swaps = [(i + k, i + 1 - k) for i in (1, 3, 5) for k in (0, 1)]
    fromacross = lax.ppermute(further, "sub", swaps)
    lanes = lax.all_gather(strips, "lane")
    extra, beside = call(faces_kernel, (shape(24, CZ), face), (src, rden, pold, cell, lanes), name="sub_faces")
    extra, cores = swap(extra, beside, "sub")
    square = shape(NS, NS, dtype=bf16)
    beside, further, subhigh, sublow, beyond, tails = call(
        dom_kernel,
        (slab, slab, face, face, shape(4, RY, CZ), shape(16, CZ)),
        (src, rden, pold, cell, slot, fromacross, extra, cores, lanes),
        [pltpu.VMEM((2, SLAB + RY + 16, CZ), f32)],
        name="dom_slabs",
    )
    fromacross, doms = swap(further, beside, "dom")
    grid = pltpu.VMEM((RX, RY, CZ), f32)
    esrc, erden, epold, xsrc, xrden, xpold, partly, kept = call(
        ring_kernel,
        (*[main] * 6, block, shape(3, 2, 4, RY, CZ)),
        (src, rden, pold, subhigh, sublow, beyond),
        [pltpu.VMEM((CX, RY, CZ), f32)] * 4,
        name="ring_fields",
    )
    pressure, hrden0, hrden1, meta, sending = call(
        first_fluid_kernel,
        (block, halo, halo, shape(48, CZ), row),
        (esrc, erden, epold, xsrc, xrden, xpold, partly, kept, doms, fromacross, tails, cell, nrm, coords, disp, slot),
        [pltpu.VMEM((8, RY, CZ), f32)] * 2 + [pltpu.VMEM((SLAB + RY + 16, CZ), f32)] * 2 + [grid] * 4,
        name="first_fluid",
    )
    received = across(sending)
    returned, mapped, khead, ktail = call(
        first_structure_kernel,
        (shape(2 * DOM, CAP * WIDE), shape(WIDE, NS), square, square),
        (received, nodes, shell),
        name="first_structure",
    )
    arrived = lax.all_to_all(returned, ("lane", "dom"), 0, 0, tiled=True)
    (values,) = call(hand_out_kernel, (shape(16, 128),), (arrived, meta), name="hand_out")
    fromacross, cores = swap(values, values, "sub")
    own_rows = shape(RX, CY, CZ)
    own0, own1 = call(own_rows_kernel, (own_rows, own_rows), (values, meta), name="own_rows")
    pressure, sending = call(
        second_fluid_kernel,
        (block, row),
        (erden, xrden, hrden0, hrden1, pressure, own0, own1, fromacross, cores, meta, cell, nrm, slot),
        [grid] * 6
        + [pltpu.VMEM((CX, CY, CZ), f32), *[pltpu.VMEM((16, 128), f32)] * 2, pltpu.SemaphoreType.DMA((4,))],
        name="second_fluid",
        far_out=(0,),
    )
    again = across(sending)
    (returned,) = call(
        second_structure_kernel, (row,), (again, received, mapped, khead, ktail, shell), name="second_structure"
    )
    arrived = across(returned)
    found, sums = call(
        arrive_kernel, (shape(WIDE, PTS), shape(SUB * LANE, 128)), (arrived, slot), name="arrive"
    )
    sums = lax.all_to_all(sums, ("sub", "lane"), 0, 0, tiled=True)
    disp_new, rms = call(finish_kernel, (shape(3, PTS), shape(1, 1)), (found, sums), name="finish")
    return pressure, disp_new, rms.reshape(())


def solution(mesh):
    every = ("dom", "sub", "lane")
    grid, points = P(*every), P(None, every)
    return jax.shard_map(
        body,
        mesh=mesh,
        in_specs=(grid, grid, grid, P(every), points, points, P(every, None), points, P(every, None), points),
        out_specs=(grid, points, P()),
        check_vma=False,
    )
```
